512 devices in a mesh: gx: 16 (over z), gy: 16 (over y, x), gz: 2 (over core).
Axes of the slice: x: 4, y: 4, z: 16, core: 2. Of those that a mesh axis runs over, the one named last changes fastest.
Arguments:
- charge: float32 [128, 256, 512], P('gx', 'gy', 'gz'), may hold values from -5 to 5
- permittivity: float32 [128, 256, 512], P('gx', 'gy', 'gz'), may hold values from 1 to 78
Outputs:
- potential: float32 [128, 256, 512], P('gx', 'gy', 'gz')
The draws below stay inside these ranges and needn't reach their ends.
All inputs are finite; a program needn't handle non-finite values.
Results may differ from the reference program's by a relative error of at most 0.00002.
Values sent between devices are 32-bit elements; how exact they have to be, the bound alone decides.
A program may use at most 64 MiB of HBM per device.

```python
import math
import jax
import jax.numpy as jnp
from jax import lax

LEVELS = 6
SWEEPS = 1
COARSE_SWEEPS = 4
NX = 128
NY = 256
NZ = 512


def draw_charge(key, part):
    key = jax.random.fold_in(key, 7)
    extent = (NX, NY, NZ)
    return jnp.clip(jax.random.normal(key, extent, jnp.float32), -5.0, 5.0)


def block_levels(key, shape, split, smallest, top_value):
    factor_of = 1.0
    for dim, shards_of in split:
        draws = jax.random.uniform(jax.random.fold_in(jax.random.fold_in(key, 6), dim), (shards_of,), jnp.float32, smallest / len(split), top_value / len(split))
        factor_of = factor_of * jnp.repeat(jnp.exp(draws), shape[dim] // shards_of).reshape((-1,) + (1,) * (len(shape) - 1 - dim))
    return factor_of


def setup_inputs(seed: int = 0) -> dict:
    arg_keys = jax.random.split(jax.random.key(seed), 3)
    return {
        "charge": draw_charge(jax.random.fold_in(arg_keys[2], 71), 0),
        "permittivity": jnp.clip(jnp.exp(math.log(78.0) - 4.356709 * jax.random.uniform(arg_keys[1], (NX, NY, NZ), jnp.float32) ** block_levels(arg_keys[1], (NX, NY, NZ), ((0, 16), (1, 16), (2, 2)), -0.2, 0.2)), 1.0, 78.0),
    }


def faces_of(padded):
    return [padded[2:, 1:-1, 1:-1], padded[:-2, 1:-1, 1:-1], padded[1:-1, 2:, 1:-1],
            padded[1:-1, :-2, 1:-1], padded[1:-1, 1:-1, 2:], padded[1:-1, 1:-1, :-2]]


def couple(field_pad, permit_pad):
    centre = permit_pad[1:-1, 1:-1, 1:-1]
    weighted = jnp.zeros(centre.shape, jnp.float32)
    conduct_sum = jnp.zeros(centre.shape, jnp.float32)
    for beside, permit_side in zip(faces_of(field_pad), faces_of(permit_pad)):
        conductance = 0.5 * (centre + permit_side)
        weighted = weighted + conductance * beside
        conduct_sum = conduct_sum + conductance
    return weighted, conduct_sum


def relax_cells(field_pad, permit_pad, source, factor, chosen):
    weighted, conduct_sum = couple(field_pad, permit_pad)
    updated = (source + factor * weighted) / (factor * conduct_sum)
    return jnp.where(chosen, updated, field_pad[1:-1, 1:-1, 1:-1])


def misfit(field_pad, permit_pad, source, factor):
    weighted, conduct_sum = couple(field_pad, permit_pad)
    return source - factor * (conduct_sum * field_pad[1:-1, 1:-1, 1:-1] - weighted)


def parity(extent, starts):
    summed = lax.broadcasted_iota(jnp.int32, extent, 0) + starts[0]
    summed = summed + lax.broadcasted_iota(jnp.int32, extent, 1) + starts[1]
    summed = summed + lax.broadcasted_iota(jnp.int32, extent, 2) + starts[2]
    return summed % 2 == 0


def coarsen(values):
    size_x, size_y, size_z = values.shape
    return values.reshape(size_x // 2, 2, size_y // 2, 2, size_z // 2, 2).mean(axis=(1, 3, 5))


def refine(values):
    return jnp.repeat(jnp.repeat(jnp.repeat(values, 2, axis=0), 2, axis=1), 2, axis=2)


def widen_zero(values):
    return jnp.pad(values, 1)


def red_black(field, permit_pad, source, factor, red_mask):
    field = relax_cells(widen_zero(field), permit_pad, source, factor, red_mask)
    return relax_cells(widen_zero(field), permit_pad, source, factor, jnp.logical_not(red_mask))


def vcycle(source, permit, level_index):
    factor = 0.25 ** level_index
    red_mask = parity(source.shape, (0, 0, 0))
    permit_pad = widen_zero(permit)
    field = jnp.zeros(source.shape, jnp.float32)
    if level_index == LEVELS - 1:
        for sweep_step in range(COARSE_SWEEPS):
            field = red_black(field, permit_pad, source, factor, red_mask)
        return field
    for sweep_step in range(SWEEPS):
        field = red_black(field, permit_pad, source, factor, red_mask)
    leftover = misfit(widen_zero(field), permit_pad, source, factor)
    field = field + refine(vcycle(coarsen(leftover), coarsen(permit), level_index + 1))
    for sweep_step in range(SWEEPS):
        field = red_black(field, permit_pad, source, factor, red_mask)
    return field


def reference(charge, permittivity):
    return vcycle(charge, permittivity, 0)
```

```python
import jax
import jax.numpy as jnp
from jax import lax
from jax.experimental import pallas as pl
from jax.experimental.pallas import tpu as pltpu
from jax.sharding import PartitionSpec as P

MESH = pl.DeviceIdType.MESH
F32 = jnp.float32
PEERS_X = 16
PEERS_Y = 16

NEAR = [(a, b, c) for c in (0, 1) for a in (-1, 0, 1) for b in (-1, 0, 1) if (a, b, c) != (0, 0, 0)]
SAME = [o for o in NEAR if o[2] == 0]
FAR = SAME + [(a, b, 0) for a in (-2, 2) for b in (-1, 0, 1)]
RING = [(i, 0, 0) for i in range(-7, 9) if i]
PLANE = [(0, i, 0) for i in range(-7, 9) if i]
GREET = sorted(set(NEAR + FAR + RING + PLANE))

COUNTS = {
    "perm1": len(NEAR), "charge0": len(NEAR), "perm0": len(NEAR), "inv1": len(NEAR), "perm2": len(FAR),
    "perm3z": len(RING), "perm3y": len(PLANE), "right1": len(NEAR), "right2": len(SAME), "right3z": len(RING),
    "right3y": len(PLANE), "late2": len(FAR),
}
BASE = {}
TOTAL = 0
for _key, _count in COUNTS.items():
    BASE[_key] = TOTAL
    TOTAL += _count


def iota(shape, dim):
    return lax.broadcasted_iota(jnp.int32, shape, dim)


def roll(value, shift, axis):
    return pltpu.roll(value, shift % value.shape[axis], axis)


def mix(left, right):
    return jnp.dot(left, right, precision=lax.Precision.HIGHEST, preferred_element_type=F32)


def halver(size, out):
    return jnp.where(iota((size, out), 0) // 2 == iota((size, out), 1), 1.0, 0.0).astype(F32)


def span(step, size, count, width):
    if step == 0:
        return pl.ds(0, size), pl.ds(0, size)
    if step > 0:
        return pl.ds(size - width, width), pl.ds(count - width, width)
    return pl.ds(0, width), pl.ds(size, width)


def kernel(
    charge_hbm, permit_hbm, out_ref,
    charge0, permit0, kx0, ky0, kz0, inv0, half0, black0, red0, stage0,
    permit1, kx1, ky1, kz1, inv1, right1, half1, black1, red1, stage1,
    permit2, kx2, ky2, kz2, right2, half2, black2, red2, late2, stage2,
    perm_col, perm_all, right_col, right_all, stage3, stage4, stage5, stage6,
    local_sem, send_sem, recv_sem,
):
    gx, gy, gz = lax.axis_index("gx"), lax.axis_index("gy"), lax.axis_index("gz")

    def peer(o):
        return (
            lax.rem(gx + (o[0] + PEERS_X), PEERS_X),
            lax.rem(gy + (o[1] + PEERS_Y), PEERS_Y),
            (1 - gz) if o[2] else gz,
        )

    copies = {}

    def send(name, index, src, dst, o):
        slot = BASE[name] + index
        copy = pltpu.make_async_remote_copy(
            src_ref=src, dst_ref=dst, send_sem=send_sem.at[slot], recv_sem=recv_sem.at[slot],
            device_id=peer(o), device_id_type=MESH,
        )
        copy.start()
        copies.setdefault(name, []).append(copy)

    def arrive(name):
        for copy in copies[name]:
            copy.wait_recv()

    barrier = pltpu.get_barrier_semaphore()
    for o in GREET:
        pl.semaphore_signal(barrier, inc=1, device_id=peer(o), device_id_type=MESH)
    own0 = (pl.ds(0, 8), pl.ds(0, 16), pl.ds(0, 256))
    fetch_permit = pltpu.make_async_copy(permit_hbm, permit0.at[own0], local_sem.at[0])
    fetch_charge = pltpu.make_async_copy(charge_hbm, charge0.at[own0], local_sem.at[1])
    fetch_permit.start()
    fetch_charge.start()
    half_256 = halver(256, 128)
    lane_half = pl.ds(pl.multiple_of(gz * 128, 128), 128)

    def coarsen0(rows):
        pairs = [rows[2 * i] + rows[2 * i + 1] for i in range(4)]
        stage0[...] = mix(jnp.concatenate(pairs, axis=0), half_256).reshape(4, 16, 128)
        return stage0[:, pl.ds(0, 8, stride=2), :] + stage0[:, pl.ds(1, 8, stride=2), :]

    fetch_permit.wait()
    permit1[pl.ds(0, 4), pl.ds(0, 8), lane_half] = 0.125 * coarsen0([permit0[i, :16, :256] for i in range(8)])
    fetch_charge.wait()
    pl.semaphore_wait(barrier, len(GREET))

    for i, o in enumerate(NEAR):
        (sx, dx), (sy, dy) = span(o[0], 4, 12, 4), span(o[1], 8, 16, 4)
        send("perm1", i, permit1.at[sx, sy, lane_half], permit1.at[dx, dy, lane_half], o)
    for name, ref, reach in (("perm0", permit0, 4), ("charge0", charge0, 3)):
        for i, o in enumerate(NEAR):
            width = reach + 1 - sum(abs(step) for step in o)
            (sx, dx), (sy, dy) = span(o[0], 8, 16, width), span(o[1], 16, 24, width)
            if o[2]:
                sz, dz = pl.ds(pl.multiple_of((1 - gz) * 128, 128), 128), pl.ds(256, 128)
            else:
                sz, dz = pl.ds(0, 256), pl.ds(0, 256)
            send(name, i, ref.at[sx, sy, sz], ref.at[dx, dy, dz], o)

    def inside_x(i, size, count):
        if i < size:
            return None
        ahead = i < (size + count) // 2
        blocks = (i - size) // size + 1 if ahead else (count - 1 - i) // size + 1
        return gx < PEERS_X - blocks if ahead else gx >= blocks

    def masked(value, i, size, count, mask):
        row_in = inside_x(i, size, count)
        keep = mask if row_in is None else jnp.logical_and(mask, row_in)
        return jnp.where(keep, value, 0.0), keep

    def inside_y(shape, own, ahead):
        row = iota(shape, 0)
        after = jnp.logical_and(jnp.logical_and(row >= own, row < ahead), gy < PEERS_Y - 1)
        return jnp.logical_or(row < own, jnp.logical_or(after, jnp.logical_and(row >= ahead, gy > 0)))

    def couplings(rows, size, count, permit, mask, kx, ky, kz, wrap):
        values = {}
        for i in rows:
            values[i] = masked(permit[i], i, size, count, mask)[0]
        shape = values[0].shape
        top = iota(shape, 1) == shape[1] - 1
        for i in rows:
            e = values[i]
            ky[i] = e + roll(e, -1, 0)
            along = e + roll(e, -1, 1)
            kz[i] = jnp.where(top, 0.0, along) if wrap else along
            after = (i + 1) % count
            if after in values:
                kx[i] = e + values[after]
        return values

    def diagonal(i, count, e, kx, ky, kz, wrap):
        y, z = ky[i], kz[i]
        total = kx[i] + kx[(i - 1) % count] + (y + roll(y, 1, 0)) + (z + roll(z, 1, 1))
        if wrap:
            lane = iota(e.shape, 1)
            ends = jnp.logical_or(lane == 0, lane == e.shape[1] - 1)
            total = total + jnp.where(ends, e, 0.0)
        return total

    def around(u, i, count, kx, ky, kz):
        here, y, z = u[i], ky[i], kz[i]
        before = (i - 1) % count
        total = kx[i] * u[(i + 1) % count] + kx[before] * u[before]
        total = total + (y * roll(here, -1, 0) + roll(y * here, 1, 0))
        return total + (z * roll(here, -1, 1) + roll(z * here, 1, 1))

    def reach(size, count, width):
        return list(range(size + width)) + list(range(count - width, count))

    arrive("perm1")
    mask1 = inside_y((16, 256), 8, 12)
    e1 = couplings(range(12), 4, 12, permit1, mask1, kx1, ky1, kz1, True)
    for i in range(4):
        inv_row = 1.0 / diagonal(i, 12, e1[i], kx1, ky1, kz1, True)
        inv1[i, pl.ds(0, 8), :] = inv_row[:8]
    for i, o in enumerate(NEAR):
        if o[2]:
            continue
        (sx, dx), (sy, dy) = span(o[0], 4, 12, 4), span(o[1], 8, 16, 4)
        send("inv1", i, inv1.at[sx, sy], inv1.at[dx, dy], o)

    def coarsen1(rows):
        half = len(rows) // 2
        pairs = [rows[2 * i] + rows[2 * i + 1] for i in range(half)]
        stage1[pl.ds(0, half)] = mix(jnp.concatenate(pairs, axis=0), half_256).reshape(half, 16, 128)
        return stage1[pl.ds(0, half), pl.ds(0, 8, stride=2), :] + stage1[pl.ds(0, half), pl.ds(1, 8, stride=2), :]

    e2 = 0.125 * coarsen1([e1[i] for i in range(12)])
    lane2 = iota((8, 128), 1)
    for i in range(2):
        e = e2[i]
        y = e + roll(e, -1, 0)
        z = jnp.where(lane2 == 127, 0.0, e + roll(e, -1, 1))
        total = (2.0 * e + e2[i + 1] + e2[(i + 5) % 6]) + (y + roll(y, 1, 0)) + (z + roll(z, 1, 1))
        total = total + jnp.where(jnp.logical_or(lane2 == 0, lane2 == 127), e, 0.0)
        permit2[0, i, pl.ds(0, 4), :] = e[:4]
        permit2[1, i, pl.ds(0, 4), :] = (1.0 / total)[:4]

    def span_far(step):
        if step == 0:
            return pl.ds(0, 2), pl.ds(0, 2)
        start = {1: 8, 2: 6, -1: 2, -2: 4}[step]
        return pl.ds(0, 2), pl.ds(start, 2)

    whole_q = pl.ds(0, 2)
    for i, o in enumerate(FAR):
        (sx, dx), (sy, dy) = span_far(o[0]), span(o[1], 4, 16, 4)
        send("perm2", i, permit2.at[whole_q, sx, sy], permit2.at[whole_q, dx, dy], o)

    z_in, z_out = iota((128, 128), 0), iota((128, 128), 1)
    pack_low = jnp.where(z_out == z_in // 2, 1.0, 0.0).astype(F32)
    pack_high = jnp.where(z_out == z_in // 2 + 64, 1.0, 0.0).astype(F32)

    def coarsen2(first, second):
        both = first + second
        low, high = both[0:1] + both[1:2], both[2:3] + both[3:4]
        return mix(low, pack_low) + mix(high, pack_high)

    perm_col[gx] = 0.125 * coarsen2(e2[0, :4], e2[1, :4])
    for i, o in enumerate(RING):
        send("perm3z", i, perm_col.at[gx], perm_col.at[gx], o)

    arrive("perm0")
    lane0 = iota((24, 384), 1)
    beside = jnp.where(gz == 0, 1, 0)
    mask_z = jnp.logical_or(
        lane0 < 256,
        jnp.logical_or(jnp.logical_and(lane0 < 320, beside == 1), jnp.logical_and(lane0 >= 320, beside == 0)),
    )
    mask0 = jnp.logical_and(inside_y((24, 384), 16, 20), mask_z)
    e0 = couplings(range(16), 8, 16, permit0, mask0, kx0, ky0, kz0, False)
    for i in reach(8, 16, 3):
        keep = masked(e0[i], i, 8, 16, mask0)[1]
        inv0[i] = jnp.where(keep, 1.0 / diagonal(i, 16, e0[i], kx0, ky0, kz0, False), 0.0)
    arrive("charge0")
    for i in reach(8, 16, 3):
        half0[i] = (2.0 * charge0[i]) * inv0[i]
    for i in reach(8, 16, 2):
        black0[i] = half0[i] + around(half0, i, 16, kx0, ky0, kz0) * inv0[i]
    odd0 = (iota((16, 256), 0) + iota((16, 256), 1)) % 2
    left0 = []
    for i in range(8):
        rest = around(black0, i, 16, kx0, ky0, kz0)[:16, :256]
        left0.append(jnp.where(odd0 == i % 2, rest, 0.0))
    right1[pl.ds(0, 4), pl.ds(0, 8), lane_half] = 0.5 * coarsen0(left0)
    for i, o in enumerate(NEAR):
        (sx, dx), (sy, dy) = span(o[0], 4, 12, 4), span(o[1], 8, 16, 4)
        send("right1", i, right1.at[sx, sy, lane_half], right1.at[dx, dy, lane_half], o)

    arrive("perm3z")
    perm_all[gy] = perm_col[...].reshape(16, 128)
    for i, o in enumerate(PLANE):
        send("perm3y", i, perm_all.at[gy], perm_all.at[gy], o)
    arrive("inv1")
    for i in reach(4, 12, 4):
        keep = masked(inv1[i], i, 4, 12, mask1)[1]
        red1[i] = jnp.where(keep, inv1[i], 0.0)
    arrive("perm2")
    mask2 = inside_y((16, 128), 4, 8)
    couplings(range(10), 2, 10, permit2.at[0], mask2, kx2, ky2, kz2, True)
    inverse2 = {}
    for i in reach(2, 10, 3):
        inverse2[i] = masked(permit2[1, i], i, 2, 10, mask2)[0]

    arrive("right1")
    for i in reach(4, 12, 4):
        half1[i] = right1[i] * red1[i]
    for i in reach(4, 12, 3):
        black1[i] = half1[i] + around(half1, i, 12, kx1, ky1, kz1) * red1[i]
    odd1 = (iota((16, 256), 0) + iota((16, 256), 1)) % 2
    left1 = []
    for i in range(4):
        left1.append(jnp.where(odd1 == i % 2, around(black1, i, 12, kx1, ky1, kz1), 0.0))
    g2 = 0.5 * coarsen1(left1)
    for i in range(2):
        right2[i, pl.ds(0, 4), :] = g2[i, :4]
        late2[0, i, pl.ds(0, 4), :] = g2[i, :4]
    for i, o in enumerate(SAME):
        sx, dx = span_far(o[0])
        sy, dy = span(o[1], 4, 16, 2)
        send("right2", i, right2.at[sx, sy], right2.at[dx, dy], o)

    arrive("perm3y")

    def ahead(u):
        return jnp.concatenate([u[1:], u[:1]], axis=0)

    def behind(u):
        return jnp.concatenate([u[-1:], u[:-1]], axis=0)

    def steps_of(extent_y, extent_x, extent_z, shape):
        y, x, z = iota(shape, 0), iota(shape, 1), iota(shape, 2)
        return [
            (ahead, y < extent_y - 1), (behind, y > 0),
            (lambda u: roll(u, -1, 1), x < extent_x - 1), (lambda u: roll(u, 1, 1), x > 0),
            (lambda u: roll(u, -1, 2), z < extent_z - 1), (lambda u: roll(u, 1, 2), z > 0),
        ]

    shape3 = (16, 16, 128)
    pair3, x3, lane3 = iota(shape3, 0), iota(shape3, 1), iota(shape3, 2)
    upper3 = lane3 >= 64
    z3 = lane3 % 64

    def across(u):
        turned = roll(u, 64, 2)
        return jnp.where(upper3, ahead(turned), behind(turned))

    steps3 = [
        (lambda u: roll(u, 64, 2), None),
        (across, jnp.logical_or(jnp.logical_and(upper3, pair3 < 15), jnp.logical_and(lane3 < 64, pair3 > 0))),
        (lambda u: roll(u, -1, 1), x3 < 15), (lambda u: roll(u, 1, 1), x3 > 0),
        (lambda u: roll(u, -1, 2), z3 < 63), (lambda u: roll(u, 1, 2), z3 > 0),
    ]

    def prepare(e, steps, cells):
        couple, total = [], None
        for shift, there in steps:
            k = e + shift(e)
            term = k if there is None else jnp.where(there, k, e)
            couple.append(k if there is None else jnp.where(there, k, 0.0))
            total = term if total is None else total + term
        inverse = 1.0 / total if cells is None else jnp.where(cells, 1.0 / total, 0.0)
        return couple, inverse

    def sum_around(u, steps, couple):
        total = None
        for (shift, _), k in zip(steps, couple):
            total = k * shift(u) if total is None else total + k * shift(u)
        return total

    pack3 = jnp.where(z_out == (z_in % 64) // 2, 1.0, 0.0).astype(F32)
    pack4 = jnp.where(z_out == z_in // 2, 1.0, 0.0).astype(F32)
    spread4 = jnp.where(jnp.logical_and(z_in == (z_out % 64) // 2, z_in < 32), 1.0, 0.0).astype(F32)
    spread5 = jnp.where(jnp.logical_and(z_in == z_out // 2, z_in < 16), 1.0, 0.0).astype(F32)

    def coarsen3(u):
        stage3[...] = mix(u.reshape(256, 128), pack3).reshape(16, 16, 128)
        return stage3[:, pl.ds(0, 8, stride=2), :] + stage3[:, pl.ds(1, 8, stride=2), :]

    def coarsen4(u):
        pairs = jnp.concatenate([u[2 * i : 2 * i + 1] + u[2 * i + 1 : 2 * i + 2] for i in range(8)], axis=0)
        stage4[...] = mix(pairs.reshape(64, 128), pack4).reshape(8, 8, 128)
        stage5[...] = jnp.zeros_like(stage5)
        stage5[:, pl.ds(0, 4), :] = stage4[:, pl.ds(0, 4, stride=2), :] + stage4[:, pl.ds(1, 4, stride=2), :]
        return stage5[...]

    shape4, shape5 = (16, 8, 128), (8, 8, 128)
    steps4, steps5 = steps_of(16, 8, 32, shape4), steps_of(8, 4, 16, shape5)
    e3 = perm_all[...]
    k3, inverse3 = prepare(e3, steps3, None)
    e4 = 0.125 * coarsen3(e3)
    k4, inverse4 = prepare(e4, steps4, iota(shape4, 2) < 32)
    e5 = 0.125 * coarsen4(e4)
    k5, inverse5 = prepare(e5, steps5, jnp.logical_and(iota(shape5, 2) < 16, iota(shape5, 1) < 4))
    even3 = (x3 + z3 + lane3 // 64) % 2 == 0
    even4 = (iota(shape4, 0) + iota(shape4, 1) + iota(shape4, 2)) % 2 == 0
    even5 = (iota(shape5, 0) + iota(shape5, 1) + iota(shape5, 2)) % 2 == 0

    arrive("right2")
    for i in reach(2, 10, 2):
        half2[i] = right2[i] * inverse2[i]
    for i in reach(2, 10, 1):
        black2[i] = half2[i] + around(half2, i, 10, kx2, ky2, kz2) * inverse2[i]
    odd2 = (iota((4, 128), 0) + iota((4, 128), 1)) % 2
    left2 = []
    for i in range(2):
        rest = around(black2, i, 10, kx2, ky2, kz2)[:4]
        left2.append(jnp.where(odd2 == i % 2, rest, 0.0))
    right_col[gx] = 0.5 * coarsen2(left2[0], left2[1])
    for i, o in enumerate(RING):
        send("right3z", i, right_col.at[gx], right_col.at[gx], o)
    for i in range(2):
        late2[1, i, pl.ds(0, 4), :] = black2[i, :4]
    for i, o in enumerate(FAR):
        (sx, dx), (sy, dy) = span_far(o[0]), span(o[1], 4, 16, 4)
        send("late2", i, late2.at[whole_q, sx, sy], late2.at[whole_q, dx, dy], o)
    arrive("right3z")
    right_all[gy] = right_col[...].reshape(16, 128)
    for i, o in enumerate(PLANE):
        send("right3y", i, right_all.at[gy], right_all.at[gy], o)
    arrive("late2")
    arrive("right3y")

    g3 = right_all[...]
    first3 = g3 * inverse3
    dark3 = (g3 + sum_around(first3, steps3, k3)) * inverse3
    rest3 = sum_around(dark3, steps3, k3)
    g4 = 0.5 * coarsen3(jnp.where(even3, rest3, 0.0))
    first4 = g4 * inverse4
    dark4 = (g4 + sum_around(first4, steps4, k4)) * inverse4
    rest4 = sum_around(dark4, steps4, k4)
    g5 = 0.5 * coarsen4(jnp.where(even4, rest4, 0.0))
    light5 = g5 * inverse5
    dark5 = (g5 + sum_around(light5, steps5, k5)) * inverse5
    for _ in range(3):
        light5 = (g5 + sum_around(dark5, steps5, k5)) * inverse5
        dark5 = (g5 + sum_around(light5, steps5, k5)) * inverse5
    u5 = jnp.where(even5, light5, dark5)
    wide5 = mix(u5.reshape(64, 128), spread5).reshape(8, 8, 128)[:, :4]
    stage4[:, pl.ds(0, 4, stride=2), :] = wide5
    stage4[:, pl.ds(1, 4, stride=2), :] = wide5
    c4 = jnp.concatenate([stage4[i // 2 : i // 2 + 1] for i in range(16)], axis=0)
    light4 = (g4 + sum_around(dark4 + c4, steps4, k4)) * inverse4
    end4 = (g4 + sum_around(light4, steps4, k4)) * inverse4
    u4 = jnp.where(even4, light4, end4)
    wide4 = mix(u4.reshape(128, 128), spread4).reshape(16, 8, 128)
    stage3[:, pl.ds(0, 8, stride=2), :] = wide4
    stage3[:, pl.ds(1, 8, stride=2), :] = wide4
    light3 = (g3 + rest3 + sum_around(stage3[...], steps3, k3)) * inverse3
    end3 = (g3 + sum_around(light3, steps3, k3)) * inverse3
    stage3[...] = jnp.where(even3, light3, end3)

    spread3 = jnp.concatenate(
        [
            jnp.where(z_in == z_out // 2, 1.0, 0.0).astype(F32),
            jnp.where(z_in == z_out // 2 + 64, 1.0, 0.0).astype(F32),
        ],
        axis=1,
    )
    for dy, base in ((0, 0), (1, 4), (-1, 12)):
        plane = stage3[lax.rem(gy + (dy + PEERS_Y), PEERS_Y)]
        turned = pltpu.roll(plane, lax.rem(PEERS_X - gx, PEERS_X), 0)
        wide = mix(turned, spread3)
        for cell, row in ((0, 0), (1, 2), (2, 4), (14, 6), (15, 8)):
            low = jnp.broadcast_to(wide[cell : cell + 1, :128], (2, 128))
            high = jnp.broadcast_to(wide[cell : cell + 1, 128:], (2, 128))
            for i in (row, row + 1):
                stage2[i, pl.ds(base, 2), :] = low
                stage2[i, pl.ds(base + 2, 2), :] = high
    for i in range(10):
        half2[i] = masked(late2[1, i] + stage2[i], i, 2, 10, mask2)[0]
    for i in reach(2, 10, 3):
        red2[i] = (late2[0, i] + around(half2, i, 10, kx2, ky2, kz2)) * inverse2[i]
    even2 = (iota((16, 128), 0) + iota((16, 128), 1)) % 2
    u2 = {}
    for i in reach(2, 10, 2):
        dark = (late2[0, i] + around(red2, i, 10, kx2, ky2, kz2)) * inverse2[i]
        u2[i] = jnp.where(even2 == i % 2, red2[i], dark)

    spread2 = jnp.where(iota((128, 256), 0) == iota((128, 256), 1) // 2, 1.0, 0.0).astype(F32)
    order2 = (0, 1, 2, 3, 8, 9)
    for j, cell in enumerate(order2):
        plane = u2[cell]
        stage1[j, pl.ds(0, 4, stride=2), :] = plane[:4]
        stage1[j, pl.ds(1, 4, stride=2), :] = plane[:4]
        for row, source in ((8, 4), (10, 5), (12, 14), (14, 15)):
            stage1[j, pl.ds(row, 2), :] = jnp.broadcast_to(plane[source : source + 1], (2, 128))
    wide2 = mix(stage1[...].reshape(96, 128), spread2)
    for j, cell in enumerate(order2):
        for i in {0: (0, 1), 1: (2, 3), 2: (4, 5), 3: (6,), 8: (9,), 9: (10, 11)}[cell]:
            half1[i] = wide2[16 * j : 16 * j + 16]
    inverse1 = {i: red1[i] for i in reach(4, 12, 2)}
    for i in reach(4, 12, 3):
        half1[i] = masked(black1[i] + half1[i], i, 4, 12, mask1)[0]
    for i in reach(4, 12, 2):
        red1[i] = (right1[i] + around(half1, i, 12, kx1, ky1, kz1)) * inverse1[i]
    u1 = {}
    for i in reach(4, 12, 1):
        dark = (right1[i] + around(red1, i, 12, kx1, ky1, kz1)) * inverse1[i]
        u1[i] = jnp.where(odd1 == i % 2, red1[i], dark)

    order1 = (0, 1, 2, 3, 4, 11)
    halo_lane = jnp.where(z_out < 64, z_out // 2, 64 + z_out // 2)
    spread_halo = jnp.where(z_in == halo_lane, 1.0, 0.0).astype(F32)
    for j, cell in enumerate(order1):
        low, high = u1[cell][:, :128], u1[cell][:, 128:]
        for part, plane in ((0, jnp.where(beside == 1, low, high)), (1, jnp.where(beside == 1, high, low))):
            stage6[part, j, pl.ds(0, 8, stride=2), :] = plane[:8]
            stage6[part, j, pl.ds(1, 8, stride=2), :] = plane[:8]
            stage6[part, j, pl.ds(16, 2), :] = jnp.broadcast_to(plane[8:9], (2, 128))
            stage6[part, j, pl.ds(22, 2), :] = jnp.broadcast_to(plane[15:16], (2, 128))
    wide1 = mix(stage6[0].reshape(144, 128), spread2)
    edge1 = mix(stage6[1].reshape(144, 128), spread_halo)
    for j, cell in enumerate(order1):
        for i in {0: (0, 1), 1: (2, 3), 2: (4, 5), 3: (6, 7), 4: (8, 9), 11: (14, 15)}[cell]:
            half0[i, :, pl.ds(0, 256)] = wide1[24 * j : 24 * j + 24]
            half0[i, :, pl.ds(256, 128)] = edge1[24 * j : 24 * j + 24]
    for i in reach(8, 16, 2):
        half0[i] = masked(black0[i] + half0[i], i, 8, 16, mask0)[0]
    for i in reach(8, 16, 1):
        red0[i] = (2.0 * charge0[i] + around(half0, i, 16, kx0, ky0, kz0)) * inv0[i]
    for i in range(8):
        dark = (2.0 * charge0[i] + around(red0, i, 16, kx0, ky0, kz0)) * inv0[i]
        out_ref[i] = jnp.where(odd0 == i % 2, red0[i, :16, :256], dark[:16, :256])

    for group in copies.values():
        for copy in group:
            copy.wait_send()


def per_device(charge, permittivity):
    def vmem(*shape):
        return pltpu.VMEM(shape, F32)

    fine, middle, coarse = (16, 24, 384), (12, 16, 256), (10, 16, 128)
    scratch = [vmem(*fine) for _ in range(9)] + [vmem(4, 16, 128)]
    scratch += [vmem(*middle) for _ in range(9)] + [vmem(6, 16, 128)]
    scratch += [vmem(2, *coarse)] + [vmem(*coarse) for _ in range(7)] + [vmem(2, *coarse), vmem(*coarse)]
    scratch += [vmem(16, 1, 128), vmem(16, 16, 128), vmem(16, 1, 128), vmem(16, 16, 128)]
    scratch += [vmem(16, 16, 128), vmem(8, 8, 128), vmem(8, 8, 128), vmem(2, 6, 24, 128)]
    scratch += [pltpu.SemaphoreType.DMA((2,)), pltpu.SemaphoreType.DMA((TOTAL,)), pltpu.SemaphoreType.DMA((TOTAL,))]
    return pl.pallas_call(
        kernel,
        out_shape=jax.ShapeDtypeStruct(charge.shape, F32),
        in_specs=[pl.BlockSpec(memory_space=pl.ANY)] * 2,
        out_specs=pl.BlockSpec(memory_space=pltpu.VMEM),
        scratch_shapes=scratch,
        compiler_params=pltpu.CompilerParams(
            collective_id=0, has_side_effects=True, vmem_limit_bytes=32 * 2**20
        ),
        name="vcycle",
    )(charge, permittivity)


def solution(mesh):
    return jax.shard_map(
        per_device,
        mesh=mesh,
        in_specs=(P("gx", "gy", "gz"), P("gx", "gy", "gz")),
        out_specs=P("gx", "gy", "gz"),
        check_vma=False,
    )
```

```python
import jax
import jax.numpy as jnp
from jax import lax
from jax.experimental import pallas as pl
from jax.experimental.pallas import tpu as pltpu
from jax.sharding import PartitionSpec as P

MESH = pl.DeviceIdType.MESH
F32 = jnp.float32
PEERS_X = 16
PEERS_Y = 16

NEAR = [(a, b, c) for c in (0, 1) for a in (-1, 0, 1) for b in (-1, 0, 1) if (a, b, c) != (0, 0, 0)]
SAME = [o for o in NEAR if o[2] == 0]
FAR = SAME + [(a, b, 0) for a in (-2, 2) for b in (-1, 0, 1)]
WIDE = NEAR + [(a, b, c) for c in (0, 1) for a in (-2, 2) for b in (-1, 0, 1)]
SIDE = [o for o in NEAR if o[0]]
RING = [(i, 0, 0) for i in range(-7, 9) if i]
PLANE = [(0, i, 0) for i in range(-7, 9) if i]

COUNTS = {
    "charge0": len(NEAR), "perm0": len(NEAR), "charge0far": len(SIDE), "perm0far": len(SIDE), "perm1": len(WIDE),
    "right1": len(WIDE), "perm2": len(FAR), "perm3z": len(RING), "perm3y": len(PLANE), "right3z": len(RING),
    "right3y": len(PLANE), "late2": len(FAR),
}
BASE = {}
TOTAL = 0
for _key, _count in COUNTS.items():
    BASE[_key] = TOTAL
    TOTAL += _count


def iota(shape, dim):
    return lax.broadcasted_iota(jnp.int32, shape, dim)


def roll(value, shift, axis):
    return pltpu.roll(value, shift % value.shape[axis], axis)


def mix(left, right):
    return jnp.dot(left, right, precision=lax.Precision.HIGHEST, preferred_element_type=F32)


def halver(size, out):
    return jnp.where(iota((size, out), 0) // 2 == iota((size, out), 1), 1.0, 0.0).astype(F32)


def span(step, size, count, width):
    if step == 0:
        return pl.ds(0, size), pl.ds(0, size)
    if step > 0:
        return pl.ds(size - width, width), pl.ds(count - width, width)
    return pl.ds(0, width), pl.ds(size, width)


def kernel(
    charge_hbm, permit_hbm, out_ref,
    charge0, permit0, kx0, ky0, kz0, inv0, half0, black0, red0, stage0, edge_permit, edge_charge,
    permit1, kx1, ky1, kz1, inv1, right1, half1, black1, red1, stage1,
    permit2, kx2, ky2, kz2, right2, half2, black2, red2, late2, stage2,
    perm_col, perm_all, right_col, right_all, stage3, stage4, stage5, stage6,
    local_sem, send_sem, recv_sem, token_sem,
):
    gx, gy, gz = lax.axis_index("gx"), lax.axis_index("gy"), lax.axis_index("gz")

    def peer(o):
        return (
            lax.rem(gx + (o[0] + PEERS_X), PEERS_X),
            lax.rem(gy + (o[1] + PEERS_Y), PEERS_Y),
            (1 - gz) if o[2] else gz,
        )

    copies = {}

    def send(name, index, src, dst, o):
        slot = BASE[name] + index
        copy = pltpu.make_async_remote_copy(
            src_ref=src, dst_ref=dst, send_sem=send_sem.at[slot], recv_sem=recv_sem.at[slot],
            device_id=peer(o), device_id_type=MESH,
        )
        copy.start()
        copies.setdefault(name, []).append(copy)

    def arrive(name):
        for copy in copies[name]:
            copy.wait_recv()

    barrier = pltpu.get_barrier_semaphore()
    for o in NEAR:
        pl.semaphore_signal(barrier, inc=1, device_id=peer(o), device_id_type=MESH)
    own0 = (pl.ds(0, 8), pl.ds(0, 16), pl.ds(0, 256))
    fetch_permit = pltpu.make_async_copy(permit_hbm, permit0.at[own0], local_sem.at[0])
    fetch_charge = pltpu.make_async_copy(charge_hbm, charge0.at[own0], local_sem.at[1])
    fetch_permit.start()
    fetch_charge.start()
    half_256 = halver(256, 128)
    lane_half = pl.ds(pl.multiple_of(gz * 128, 128), 128)

    def coarsen0(rows):
        pairs = [rows[2 * i] + rows[2 * i + 1] for i in range(4)]
        stage0[...] = mix(jnp.concatenate(pairs, axis=0), half_256).reshape(4, 16, 128)
        return stage0[:, pl.ds(0, 8, stride=2), :] + stage0[:, pl.ds(1, 8, stride=2), :]

    def tell(turn):
        step = 2**turn
        for o in ((step, 0, 0), (-step, 0, 0), (0, step, 0), (0, -step, 0)):
            pl.semaphore_signal(token_sem.at[turn], inc=1, device_id=peer(o), device_id_type=MESH)

    def hear(turn):
        pl.semaphore_wait(token_sem.at[turn], 4)

    def send0(name, source, ref, reach, far):
        for i, o in enumerate(SIDE if far else NEAR):
            away = sum(abs(step) for step in o)
            width = reach + 1 - away
            sx, dx, target = pl.ds(0, 8), pl.ds(0, 8), ref
            if far and away == 3:
                continue
            if o[0]:
                last = 1 if away < 3 else 0
                rows = 1 if far else width - last
                start = (width - 1 if far else 0) if o[0] < 0 else 8 - (width if far else width - last)
                sx, dx = pl.ds(start, rows), pl.ds(start + 8, rows)
                if far and away == 2:
                    target, dx = (edge_permit if reach == 4 else edge_charge), pl.ds(0 if o[0] < 0 else 1, 1)
            sy, dy = span(o[1], 16, 24, width)
            if o[2]:
                sz, dz = pl.ds(pl.multiple_of((1 - gz) * 128, 128), 128), pl.ds(256, 128)
            else:
                sz, dz = pl.ds(0, 256), pl.ds(0, 256)
            send(name, i, source.at[sx, sy, sz], target.at[dx, dy, dz], o)

    pl.semaphore_wait(barrier, len(NEAR))
    tell(0)
    send0("perm0", permit_hbm, permit0, 4, False)
    send0("charge0", charge_hbm, charge0, 3, False)

    fetch_permit.wait()
    permit1[pl.ds(0, 4), pl.ds(0, 8), lane_half] = 0.125 * coarsen0([permit0[i, :16, :256] for i in range(8)])
    fetch_charge.wait()

    def send1(name, ref, reach, peers):
        for i, o in enumerate(WIDE):
            if o not in peers:
                continue
            away = abs(o[0])
            along = {0: 4, 1: 4, 2: reach - 4 - abs(o[1])}[away]
            across = {0: reach, 1: reach - 1, 2: reach - 5}[away]
            if away < 2:
                sx, dx = span(o[0], 4, 18, along)
            else:
                sx = pl.ds(4 - along, along) if o[0] > 0 else pl.ds(0, along)
                dx = pl.ds(14 - along, along) if o[0] > 0 else pl.ds(8, along)
            sy, dy = span(o[1], 8, 24, across)
            send(name, i, ref.at[sx, sy, lane_half], ref.at[dx, dy, lane_half], o)

    send1("perm1", permit1, 7, NEAR)
    hear(0)
    tell(1)
    send1("perm1", permit1, 7, WIDE[len(NEAR):])
    send0("perm0far", permit_hbm, permit0, 4, True)
    send0("charge0far", charge_hbm, charge0, 3, True)

    def inside_x(i, size, count):
        if i < size:
            return None
        ahead = i < (size + count) // 2
        blocks = (i - size) // size + 1 if ahead else (count - 1 - i) // size + 1
        return gx < PEERS_X - blocks if ahead else gx >= blocks

    def masked(value, i, size, count, mask):
        row_in = inside_x(i, size, count)
        keep = mask if row_in is None else jnp.logical_and(mask, row_in)
        return jnp.where(keep, value, 0.0), keep

    def inside_y(shape, own, ahead):
        row = iota(shape, 0)
        after = jnp.logical_and(jnp.logical_and(row >= own, row < ahead), gy < PEERS_Y - 1)
        return jnp.logical_or(row < own, jnp.logical_or(after, jnp.logical_and(row >= ahead, gy > 0)))

    def couplings(rows, size, count, permit, mask, kx, ky, kz, wrap):
        values = {}
        for i in rows:
            values[i] = masked(permit[i], i, size, count, mask)[0]
        shape = values[rows[0]].shape
        top = iota(shape, 1) == shape[1] - 1
        for i in rows:
            e = values[i]
            ky[i] = e + roll(e, -1, 0)
            along = e + roll(e, -1, 1)
            kz[i] = jnp.where(top, 0.0, along) if wrap else along
            after = (i + 1) % count
            if after in values:
                kx[i] = e + values[after]
        return values

    def diagonal(i, count, e, kx, ky, kz, wrap):
        y, z = ky[i], kz[i]
        total = kx[i] + kx[(i - 1) % count] + (y + roll(y, 1, 0)) + (z + roll(z, 1, 1))
        if wrap:
            lane = iota(e.shape, 1)
            ends = jnp.logical_or(lane == 0, lane == e.shape[1] - 1)
            total = total + jnp.where(ends, e, 0.0)
        return total

    def around(u, i, count, kx, ky, kz):
        here, y, z = u[i], ky[i], kz[i]
        before = (i - 1) % count
        total = kx[i] * u[(i + 1) % count] + kx[before] * u[before]
        total = total + (y * roll(here, -1, 0) + roll(y * here, 1, 0))
        return total + (z * roll(here, -1, 1) + roll(z * here, 1, 1))

    def reach(size, count, width):
        return list(range(size + width)) + list(range(count - width, count))

    hear(1)
    tell(2)

    arrive("perm0")
    lane0 = iota((24, 384), 1)
    beside = jnp.where(gz == 0, 1, 0)
    mask_z = jnp.logical_or(
        lane0 < 256,
        jnp.logical_or(jnp.logical_and(lane0 < 320, beside == 1), jnp.logical_and(lane0 >= 320, beside == 0)),
    )
    mask0 = jnp.logical_and(inside_y((24, 384), 16, 20), mask_z)
    e0 = couplings(reach(8, 16, 3), 8, 16, permit0, mask0, kx0, ky0, kz0, False)

    def diagonal0(i, e):
        keep = masked(e, i, 8, 16, mask0)[1]
        inv0[i] = jnp.where(keep, 1.0 / diagonal(i, 16, e, kx0, ky0, kz0, False), 0.0)

    def first0(i, charge):
        half0[i] = (2.0 * charge) * inv0[i]

    def second0(i):
        black0[i] = half0[i] + around(half0, i, 16, kx0, ky0, kz0) * inv0[i]

    for i in reach(8, 16, 2):
        diagonal0(i, e0[i])
    arrive("charge0")
    for i in reach(8, 16, 2):
        first0(i, charge0[i])
    for i in reach(8, 16, 1):
        second0(i)
    odd0 = (iota((16, 256), 0) + iota((16, 256), 1)) % 2
    left0 = []
    for i in range(8):
        rest = around(black0, i, 16, kx0, ky0, kz0)[:16, :256]
        left0.append(jnp.where(odd0 == i % 2, rest, 0.0))
    right1[pl.ds(0, 4), pl.ds(0, 8), lane_half] = 0.5 * coarsen0(left0)
    send1("right1", right1, 6, WIDE)

    arrive("perm1")
    mask1 = inside_y((24, 256), 8, 16)
    e1 = couplings(range(18), 4, 18, permit1, mask1, kx1, ky1, kz1, True)

    def coarsen1(rows, ref, cells):
        half = len(rows) // 2
        pairs = [rows[2 * i] + rows[2 * i + 1] for i in range(half)]
        stage1[pl.ds(0, half)] = mix(jnp.concatenate(pairs, axis=0), half_256).reshape(half, 24, 128)
        for j, cell in enumerate(cells):
            ref[cell, pl.ds(0, 8), :] = stage1[j, pl.ds(0, 8, stride=2), :] + stage1[j, pl.ds(1, 8, stride=2), :]
            ref[cell, pl.ds(12, 4), :] = stage1[j, pl.ds(16, 4, stride=2), :] + stage1[j, pl.ds(17, 4, stride=2), :]

    cells2 = (0, 1, 2, 3, 4, 7, 8, 9)
    coarsen1([0.125 * e1[i] for i in (0, 1, 2, 3, 4, 5, 6, 7, 8, 9, 12, 13, 14, 15, 16, 17)], stage2, cells2)
    mask2 = inside_y((16, 128), 4, 8)
    e2 = couplings(cells2, 2, 10, stage2, mask2, kx2, ky2, kz2, True)
    inverse2 = {}
    for i in reach(2, 10, 2):
        keep = masked(e2[i], i, 2, 10, mask2)[1]
        inverse2[i] = jnp.where(keep, 1.0 / diagonal(i, 10, e2[i], kx2, ky2, kz2, True), 0.0)
    for i in range(2):
        permit2[0, i, pl.ds(0, 4), :] = e2[i][:4]
        permit2[1, i, pl.ds(0, 4), :] = inverse2[i][:4]

    z_in, z_out = iota((128, 128), 0), iota((128, 128), 1)
    pack_low = jnp.where(z_out == z_in // 2, 1.0, 0.0).astype(F32)
    pack_high = jnp.where(z_out == z_in // 2 + 64, 1.0, 0.0).astype(F32)

    def coarsen2(first, second):
        both = first + second
        low, high = both[0:1] + both[1:2], both[2:3] + both[3:4]
        return mix(low, pack_low) + mix(high, pack_high)

    hear(2)
    perm_col[gx] = 0.125 * coarsen2(e2[0][:4], e2[1][:4])
    for i, o in enumerate(RING):
        send("perm3z", i, perm_col.at[gx], perm_col.at[gx], o)

    def span_far(step):
        if step == 0:
            return pl.ds(0, 2), pl.ds(0, 2)
        start = {1: 8, 2: 6, -1: 2, -2: 4}[step]
        return pl.ds(0, 2), pl.ds(start, 2)

    whole_q = pl.ds(0, 2)
    for i, o in enumerate(FAR):
        (sx, dx), (sy, dy) = span_far(o[0]), span(o[1], 4, 16, 4)
        send("perm2", i, permit2.at[whole_q, sx, sy], permit2.at[whole_q, dx, dy], o)
    for i in reach(4, 18, 6):
        keep = masked(e1[i], i, 4, 18, mask1)[1]
        inv1[i] = jnp.where(keep, 1.0 / diagonal(i, 18, e1[i], kx1, ky1, kz1, True), 0.0)

    arrive("perm0far")
    arrive("charge0far")
    edge = jnp.logical_or(iota((24, 384), 0) >= 16, lane0 >= 256)
    far_permit = {i: permit0[i] for i in range(8, 16)}
    far_permit[10] = jnp.where(edge, edge_permit[0], far_permit[10])
    far_permit[13] = jnp.where(edge, edge_permit[1], far_permit[13])
    far_charge = {i: charge0[i] for i in (8, 9, 10, 13, 14, 15)}
    far_charge[9] = jnp.where(edge, edge_charge[0], far_charge[9])
    far_charge[14] = jnp.where(edge, edge_charge[1], far_charge[14])
    e0 = couplings(range(8, 16), 8, 16, far_permit, mask0, kx0, ky0, kz0, False)
    for i in (8, 9, 10, 13, 14, 15):
        diagonal0(i, e0[i])
    for i in (8, 9, 10, 13, 14, 15):
        first0(i, far_charge[i])
    for i in (8, 9, 14, 15):
        second0(i)

    arrive("right1")
    for i in reach(4, 18, 6):
        half1[i] = right1[i] * inv1[i]
    for i in reach(4, 18, 5):
        black1[i] = half1[i] + around(half1, i, 18, kx1, ky1, kz1) * inv1[i]
    odd1 = (iota((24, 256), 0) + iota((24, 256), 1)) % 2
    left1 = []
    for i in reach(4, 18, 4):
        left1.append(jnp.where(odd1 == i % 2, 0.5 * around(black1, i, 18, kx1, ky1, kz1), 0.0))
    coarsen1(left1, right2, (0, 1, 2, 3, 8, 9))

    for i in reach(2, 10, 2):
        half2[i] = right2[i] * inverse2[i]
    for i in reach(2, 10, 1):
        black2[i] = half2[i] + around(half2, i, 10, kx2, ky2, kz2) * inverse2[i]
    odd2 = (iota((4, 128), 0) + iota((4, 128), 1)) % 2
    left2 = []
    for i in range(2):
        rest = around(black2, i, 10, kx2, ky2, kz2)[:4]
        left2.append(jnp.where(odd2 == i % 2, rest, 0.0))
    right_col[gx] = 0.5 * coarsen2(left2[0], left2[1])
    for i, o in enumerate(RING):
        send("right3z", i, right_col.at[gx], right_col.at[gx], o)
    for i in range(2):
        late2[0, i, pl.ds(0, 4), :] = right2[i, :4]
        late2[1, i, pl.ds(0, 4), :] = black2[i, :4]
    for i, o in enumerate(FAR):
        (sx, dx), (sy, dy) = span_far(o[0]), span(o[1], 4, 16, 4)
        send("late2", i, late2.at[whole_q, sx, sy], late2.at[whole_q, dx, dy], o)

    arrive("perm3z")
    perm_all[gy] = perm_col[...].reshape(16, 128)
    for i, o in enumerate(PLANE):
        send("perm3y", i, perm_all.at[gy], perm_all.at[gy], o)
    arrive("perm2")
    couplings(range(10), 2, 10, permit2.at[0], mask2, kx2, ky2, kz2, True)
    for i in reach(2, 10, 3):
        inverse2[i] = masked(permit2[1, i], i, 2, 10, mask2)[0]

    arrive("perm3y")

    def ahead(u):
        return jnp.concatenate([u[1:], u[:1]], axis=0)

    def behind(u):
        return jnp.concatenate([u[-1:], u[:-1]], axis=0)

    def steps_of(extent_y, extent_x, extent_z, shape):
        y, x, z = iota(shape, 0), iota(shape, 1), iota(shape, 2)
        return [
            (ahead, y < extent_y - 1), (behind, y > 0),
            (lambda u: roll(u, -1, 1), x < extent_x - 1), (lambda u: roll(u, 1, 1), x > 0),
            (lambda u: roll(u, -1, 2), z < extent_z - 1), (lambda u: roll(u, 1, 2), z > 0),
        ]

    shape3 = (16, 16, 128)
    pair3, x3, lane3 = iota(shape3, 0), iota(shape3, 1), iota(shape3, 2)
    upper3 = lane3 >= 64
    z3 = lane3 % 64

    def across(u):
        turned = roll(u, 64, 2)
        return jnp.where(upper3, ahead(turned), behind(turned))

    steps3 = [
        (lambda u: roll(u, 64, 2), None),
        (across, jnp.logical_or(jnp.logical_and(upper3, pair3 < 15), jnp.logical_and(lane3 < 64, pair3 > 0))),
        (lambda u: roll(u, -1, 1), x3 < 15), (lambda u: roll(u, 1, 1), x3 > 0),
        (lambda u: roll(u, -1, 2), z3 < 63), (lambda u: roll(u, 1, 2), z3 > 0),
    ]

    def prepare(e, steps, cells):
        couple, total = [], None
        for shift, there in steps:
            k = e + shift(e)
            term = k if there is None else jnp.where(there, k, e)
            couple.append(k if there is None else jnp.where(there, k, 0.0))
            total = term if total is None else total + term
        inverse = 1.0 / total if cells is None else jnp.where(cells, 1.0 / total, 0.0)
        return couple, inverse

    def sum_around(u, steps, couple):
        total = None
        for (shift, _), k in zip(steps, couple):
            total = k * shift(u) if total is None else total + k * shift(u)
        return total

    pack3 = jnp.where(z_out == (z_in % 64) // 2, 1.0, 0.0).astype(F32)
    pack4 = jnp.where(z_out == z_in // 2, 1.0, 0.0).astype(F32)
    spread4 = jnp.where(jnp.logical_and(z_in == (z_out % 64) // 2, z_in < 32), 1.0, 0.0).astype(F32)
    spread5 = jnp.where(jnp.logical_and(z_in == z_out // 2, z_in < 16), 1.0, 0.0).astype(F32)

    def coarsen3(u):
        stage3[...] = mix(u.reshape(256, 128), pack3).reshape(16, 16, 128)
        return stage3[:, pl.ds(0, 8, stride=2), :] + stage3[:, pl.ds(1, 8, stride=2), :]

    def coarsen4(u):
        pairs = jnp.concatenate([u[2 * i : 2 * i + 1] + u[2 * i + 1 : 2 * i + 2] for i in range(8)], axis=0)
        stage4[...] = mix(pairs.reshape(64, 128), pack4).reshape(8, 8, 128)
        stage5[...] = jnp.zeros_like(stage5)
        stage5[:, pl.ds(0, 4), :] = stage4[:, pl.ds(0, 4, stride=2), :] + stage4[:, pl.ds(1, 4, stride=2), :]
        return stage5[...]

    shape4, shape5 = (16, 8, 128), (8, 8, 128)
    steps4, steps5 = steps_of(16, 8, 32, shape4), steps_of(8, 4, 16, shape5)
    e3 = perm_all[...]
    k3, inverse3 = prepare(e3, steps3, None)
    e4 = 0.125 * coarsen3(e3)
    k4, inverse4 = prepare(e4, steps4, iota(shape4, 2) < 32)
    e5 = 0.125 * coarsen4(e4)
    k5, inverse5 = prepare(e5, steps5, jnp.logical_and(iota(shape5, 2) < 16, iota(shape5, 1) < 4))
    even3 = (x3 + z3 + lane3 // 64) % 2 == 0
    even4 = (iota(shape4, 0) + iota(shape4, 1) + iota(shape4, 2)) % 2 == 0
    even5 = (iota(shape5, 0) + iota(shape5, 1) + iota(shape5, 2)) % 2 == 0

    arrive("right3z")
    right_all[gy] = right_col[...].reshape(16, 128)
    for i, o in enumerate(PLANE):
        send("right3y", i, right_all.at[gy], right_all.at[gy], o)
    arrive("late2")
    arrive("right3y")

    g3 = right_all[...]
    first3 = g3 * inverse3
    dark3 = (g3 + sum_around(first3, steps3, k3)) * inverse3
    rest3 = sum_around(dark3, steps3, k3)
    g4 = 0.5 * coarsen3(jnp.where(even3, rest3, 0.0))
    first4 = g4 * inverse4
    dark4 = (g4 + sum_around(first4, steps4, k4)) * inverse4
    rest4 = sum_around(dark4, steps4, k4)
    g5 = 0.5 * coarsen4(jnp.where(even4, rest4, 0.0))
    light5 = g5 * inverse5
    dark5 = (g5 + sum_around(light5, steps5, k5)) * inverse5
    for _ in range(3):
        light5 = (g5 + sum_around(dark5, steps5, k5)) * inverse5
        dark5 = (g5 + sum_around(light5, steps5, k5)) * inverse5
    u5 = jnp.where(even5, light5, dark5)
    wide5 = mix(u5.reshape(64, 128), spread5).reshape(8, 8, 128)[:, :4]
    stage4[:, pl.ds(0, 4, stride=2), :] = wide5
    stage4[:, pl.ds(1, 4, stride=2), :] = wide5
    c4 = jnp.concatenate([stage4[i // 2 : i // 2 + 1] for i in range(16)], axis=0)
    light4 = (g4 + sum_around(dark4 + c4, steps4, k4)) * inverse4
    end4 = (g4 + sum_around(light4, steps4, k4)) * inverse4
    u4 = jnp.where(even4, light4, end4)
    wide4 = mix(u4.reshape(128, 128), spread4).reshape(16, 8, 128)
    stage3[:, pl.ds(0, 8, stride=2), :] = wide4
    stage3[:, pl.ds(1, 8, stride=2), :] = wide4
    light3 = (g3 + rest3 + sum_around(stage3[...], steps3, k3)) * inverse3
    end3 = (g3 + sum_around(light3, steps3, k3)) * inverse3
    stage3[...] = jnp.where(even3, light3, end3)

    spread3 = jnp.concatenate(
        [
            jnp.where(z_in == z_out // 2, 1.0, 0.0).astype(F32),
            jnp.where(z_in == z_out // 2 + 64, 1.0, 0.0).astype(F32),
        ],
        axis=1,
    )
    for dy, base in ((0, 0), (1, 4), (-1, 12)):
        plane = stage3[lax.rem(gy + (dy + PEERS_Y), PEERS_Y)]
        turned = pltpu.roll(plane, lax.rem(PEERS_X - gx, PEERS_X), 0)
        wide = mix(turned, spread3)
        for cell, row in ((0, 0), (1, 2), (2, 4), (14, 6), (15, 8)):
            low = jnp.broadcast_to(wide[cell : cell + 1, :128], (2, 128))
            high = jnp.broadcast_to(wide[cell : cell + 1, 128:], (2, 128))
            for i in (row, row + 1):
                stage2[i, pl.ds(base, 2), :] = low
                stage2[i, pl.ds(base + 2, 2), :] = high
    for i in range(10):
        half2[i] = masked(late2[1, i] + stage2[i], i, 2, 10, mask2)[0]
    for i in reach(2, 10, 3):
        red2[i] = (late2[0, i] + around(half2, i, 10, kx2, ky2, kz2)) * inverse2[i]
    even2 = (iota((16, 128), 0) + iota((16, 128), 1)) % 2
    u2 = {}
    for i in reach(2, 10, 2):
        dark = (late2[0, i] + around(red2, i, 10, kx2, ky2, kz2)) * inverse2[i]
        u2[i] = jnp.where(even2 == i % 2, red2[i], dark)

    spread2 = jnp.where(iota((128, 256), 0) == iota((128, 256), 1) // 2, 1.0, 0.0).astype(F32)
    order2 = (0, 1, 2, 3, 8, 9)
    for j, cell in enumerate(order2):
        plane = u2[cell]
        stage1[j, pl.ds(0, 4, stride=2), :] = plane[:4]
        stage1[j, pl.ds(1, 4, stride=2), :] = plane[:4]
        for row, source in ((8, 4), (10, 5), (20, 14), (22, 15)):
            stage1[j, pl.ds(row, 2), :] = jnp.broadcast_to(plane[source : source + 1], (2, 128))
    wide2 = mix(stage1[pl.ds(0, 6)].reshape(144, 128), spread2)
    for j, cell in enumerate(order2):
        for i in {0: (0, 1), 1: (2, 3), 2: (4, 5), 3: (6,), 8: (15,), 9: (16, 17)}[cell]:
            part = black1[i] + wide2[24 * j : 24 * j + 24]
            half1[i] = masked(part, i, 4, 18, mask1)[0]
    for i in reach(4, 18, 2):
        red1[i] = (right1[i] + around(half1, i, 18, kx1, ky1, kz1)) * inv1[i]
    u1 = {}
    for i in reach(4, 18, 1):
        dark = (right1[i] + around(red1, i, 18, kx1, ky1, kz1)) * inv1[i]
        u1[i] = jnp.where(odd1 == i % 2, red1[i], dark)

    order1 = (0, 1, 2, 3, 4, 17)
    halo_lane = jnp.where(z_out < 64, z_out // 2, 64 + z_out // 2)
    spread_halo = jnp.where(z_in == halo_lane, 1.0, 0.0).astype(F32)
    for j, cell in enumerate(order1):
        low, high = u1[cell][:, :128], u1[cell][:, 128:]
        for part, plane in ((0, jnp.where(beside == 1, low, high)), (1, jnp.where(beside == 1, high, low))):
            stage6[part, j, pl.ds(0, 8, stride=2), :] = plane[:8]
            stage6[part, j, pl.ds(1, 8, stride=2), :] = plane[:8]
            stage6[part, j, pl.ds(16, 2), :] = jnp.broadcast_to(plane[8:9], (2, 128))
            stage6[part, j, pl.ds(22, 2), :] = jnp.broadcast_to(plane[23:24], (2, 128))
    wide1 = mix(stage6[0].reshape(144, 128), spread2)
    edge1 = mix(stage6[1].reshape(144, 128), spread_halo)
    for j, cell in enumerate(order1):
        for i in {0: (0, 1), 1: (2, 3), 2: (4, 5), 3: (6, 7), 4: (8, 9), 17: (14, 15)}[cell]:
            part = jnp.concatenate([wide1[24 * j : 24 * j + 24], edge1[24 * j : 24 * j + 24]], axis=1)
            half0[i] = masked(black0[i] + part, i, 8, 16, mask0)[0]
    for i in reach(8, 16, 1):
        red0[i] = (2.0 * charge0[i] + around(half0, i, 16, kx0, ky0, kz0)) * inv0[i]
    for i in range(8):
        dark = (2.0 * charge0[i] + around(red0, i, 16, kx0, ky0, kz0)) * inv0[i]
        out_ref[i] = jnp.where(odd0 == i % 2, red0[i, :16, :256], dark[:16, :256])

    for group in copies.values():
        for copy in group:
            copy.wait_send()


def per_device(charge, permittivity):
    def vmem(*shape):
        return pltpu.VMEM(shape, F32)

    fine, middle, coarse = (16, 24, 384), (18, 24, 256), (10, 16, 128)
    scratch = [vmem(*fine) for _ in range(9)] + [vmem(4, 16, 128), vmem(2, 24, 384), vmem(2, 24, 384)]
    scratch += [vmem(*middle) for _ in range(9)] + [vmem(8, 24, 128)]
    scratch += [vmem(2, *coarse)] + [vmem(*coarse) for _ in range(7)] + [vmem(2, *coarse), vmem(*coarse)]
    scratch += [vmem(16, 1, 128), vmem(16, 16, 128), vmem(16, 1, 128), vmem(16, 16, 128)]
    scratch += [vmem(16, 16, 128), vmem(8, 8, 128), vmem(8, 8, 128), vmem(2, 6, 24, 128)]
    scratch += [pltpu.SemaphoreType.DMA((2,)), pltpu.SemaphoreType.DMA((TOTAL,)), pltpu.SemaphoreType.DMA((TOTAL,))]
    scratch += [pltpu.SemaphoreType.REGULAR((3,))]
    return pl.pallas_call(
        kernel,
        out_shape=jax.ShapeDtypeStruct(charge.shape, F32),
        in_specs=[pl.BlockSpec(memory_space=pl.ANY)] * 2,
        out_specs=pl.BlockSpec(memory_space=pltpu.VMEM),
        scratch_shapes=scratch,
        compiler_params=pltpu.CompilerParams(
            collective_id=0, has_side_effects=True, vmem_limit_bytes=60 * 2**20
        ),
        name="vcycle",
    )(charge, permittivity)


def solution(mesh):
    return jax.shard_map(
        per_device,
        mesh=mesh,
        in_specs=(P("gx", "gy", "gz"), P("gx", "gy", "gz")),
        out_specs=P("gx", "gy", "gz"),
        check_vma=False,
    )
```

```python
import jax
import jax.numpy as jnp
from jax import lax
from jax.experimental import pallas as pl
from jax.experimental.pallas import tpu as pltpu
from jax.sharding import PartitionSpec as P

MESH = pl.DeviceIdType.MESH
F32 = jnp.float32
PEERS_X = 16
PEERS_Y = 16

NEAR = [(a, b, c) for c in (0, 1) for a in (-1, 0, 1) for b in (-1, 0, 1) if (a, b, c) != (0, 0, 0)]
SAME = [o for o in NEAR if o[2] == 0]
FAR = SAME + [(a, b, 0) for a in (-2, 2) for b in (-1, 0, 1)]
WIDE = NEAR + [(a, b, c) for c in (0, 1) for a in (-2, 2) for b in (-1, 0, 1)]
SIDE = [o for o in NEAR if o[0]]
RING = [(i, 0, 0) for i in range(-7, 9) if i]
PLANE = [(0, i, 0) for i in range(-7, 9) if i]

COUNTS = {
    "charge0": len(NEAR), "perm0": len(NEAR), "charge0far": len(SIDE), "perm0far": len(SIDE), "perm1": len(WIDE),
    "right1": len(WIDE), "perm2": len(FAR), "perm3z": len(RING), "perm3y": len(PLANE), "right3z": len(RING),
    "right3y": len(PLANE), "late2": len(FAR),
}
BASE = {}
TOTAL = 0
for _key, _count in COUNTS.items():
    BASE[_key] = TOTAL
    TOTAL += _count


def iota(shape, dim):
    return lax.broadcasted_iota(jnp.int32, shape, dim)


def roll(value, shift, axis):
    return pltpu.roll(value, shift % value.shape[axis], axis)


def mix(left, right):
    if left.shape[0] % 16:
        return jnp.dot(left, right, precision=lax.Precision.HIGHEST, preferred_element_type=F32)
    ones, total = right.astype(jnp.bfloat16), None
    for _ in range(3):
        part = left.astype(jnp.bfloat16)
        left = left - part.astype(F32)
        term = jnp.dot(part, ones, preferred_element_type=F32)
        total = term if total is None else total + term
    return total


def halver(size, out):
    return jnp.where(iota((size, out), 0) // 2 == iota((size, out), 1), 1.0, 0.0).astype(F32)


def span(step, size, count, width):
    if step == 0:
        return pl.ds(0, size), pl.ds(0, size)
    if step > 0:
        return pl.ds(size - width, width), pl.ds(count - width, width)
    return pl.ds(0, width), pl.ds(size, width)


def kernel(
    charge_hbm, permit_hbm, out_ref,
    charge0, permit0, kx0, ky0, kz0, inv0, half0, black0, red0, stage0, edge_permit, edge_charge,
    permit1, kx1, ky1, kz1, inv1, right1, half1, black1, red1, stage1,
    permit2, kx2, ky2, kz2, right2, half2, black2, red2, late2, stage2,
    perm_col, perm_all, right_col, right_all, stage3, stage4, stage5, stage6, couple3, up3, up4,
    local_sem, send_sem, recv_sem, token_sem,
):
    gx, gy, gz = lax.axis_index("gx"), lax.axis_index("gy"), lax.axis_index("gz")

    def peer(o):
        return (
            lax.rem(gx + (o[0] + PEERS_X), PEERS_X),
            lax.rem(gy + (o[1] + PEERS_Y), PEERS_Y),
            (1 - gz) if o[2] else gz,
        )

    copies = {}

    def send(name, index, src, dst, o):
        slot = BASE[name] + index
        copy = pltpu.make_async_remote_copy(
            src_ref=src, dst_ref=dst, send_sem=send_sem.at[slot], recv_sem=recv_sem.at[slot],
            device_id=peer(o), device_id_type=MESH,
        )
        copy.start()
        copies.setdefault(name, []).append(copy)

    def arrive(name, skip=None):
        for index, copy in enumerate(copies[name]):
            if index != skip:
                copy.wait_recv()

    barrier = pltpu.get_barrier_semaphore()
    for o in NEAR:
        pl.semaphore_signal(barrier, inc=1, device_id=peer(o), device_id_type=MESH)
    own0 = (pl.ds(0, 8), pl.ds(0, 16), pl.ds(0, 256))
    fetch_permit = pltpu.make_async_copy(permit_hbm, permit0.at[own0], local_sem.at[0])
    fetch_charge = pltpu.make_async_copy(charge_hbm, charge0.at[own0], local_sem.at[1])
    fetch_permit.start()
    fetch_charge.start()
    half_256 = halver(256, 128)
    lane_half = pl.ds(pl.multiple_of(gz * 128, 128), 128)

    def coarsen0(rows):
        pairs = [rows[2 * i] + rows[2 * i + 1] for i in range(4)]
        stage0[...] = mix(jnp.concatenate(pairs, axis=0), half_256).reshape(4, 16, 128)
        return stage0[:, pl.ds(0, 8, stride=2), :] + stage0[:, pl.ds(1, 8, stride=2), :]

    def tell(turn):
        step = 2**turn
        for o in ((step, 0, 0), (-step, 0, 0), (0, step, 0), (0, -step, 0)):
            pl.semaphore_signal(token_sem.at[turn], inc=1, device_id=peer(o), device_id_type=MESH)

    def hear(turn):
        pl.semaphore_wait(token_sem.at[turn], 4)

    def send0(name, source, ref, reach, far):
        for i, o in enumerate(SIDE if far else NEAR):
            away = sum(abs(step) for step in o)
            width = reach + 1 - away
            sx, dx, target = pl.ds(0, 8), pl.ds(0, 8), ref
            if far and away == 3:
                continue
            if o[0]:
                last = 1 if away < 3 else 0
                rows = 1 if far else width - last
                start = (width - 1 if far else 0) if o[0] < 0 else 8 - (width if far else width - last)
                sx, dx = pl.ds(start, rows), pl.ds(start + 8, rows)
                if far and away == 2:
                    target, dx = (edge_permit if reach == 4 else edge_charge), pl.ds(0 if o[0] < 0 else 1, 1)
            sy, dy = span(o[1], 16, 24, width)
            if o[2]:
                sz, dz = pl.ds(pl.multiple_of((1 - gz) * 128, 128), 128), pl.ds(256, 128)
            else:
                sz, dz = pl.ds(0, 256), pl.ds(0, 256)
            send(name, i, source.at[sx, sy, sz], target.at[dx, dy, dz], o)

    pl.semaphore_wait(barrier, len(NEAR))
    tell(0)
    send0("perm0", permit_hbm, permit0, 4, False)
    send0("charge0", charge_hbm, charge0, 3, False)

    fetch_permit.wait()
    permit1[pl.ds(0, 4), pl.ds(0, 8), lane_half] = 0.125 * coarsen0([permit0[i, :16, :256] for i in range(8)])
    fetch_charge.wait()

    def send1(name, ref, reach, peers):
        for i, o in enumerate(WIDE):
            if o not in peers:
                continue
            away = abs(o[0])
            along = {0: 4, 1: 4, 2: reach - 4 - abs(o[1])}[away]
            across = {0: reach, 1: reach - 1, 2: reach - 5}[away]
            if away < 2:
                sx, dx = span(o[0], 4, 18, along)
            else:
                sx = pl.ds(4 - along, along) if o[0] > 0 else pl.ds(0, along)
                dx = pl.ds(14 - along, along) if o[0] > 0 else pl.ds(8, along)
            sy, dy = span(o[1], 8, 24, across)
            send(name, i, ref.at[sx, sy, lane_half], ref.at[dx, dy, lane_half], o)

    send1("perm1", permit1, 7, NEAR)
    hear(0)
    tell(1)
    send1("perm1", permit1, 7, WIDE[len(NEAR):])
    send0("perm0far", permit_hbm, permit0, 4, True)
    send0("charge0far", charge_hbm, charge0, 3, True)

    def inside_x(i, size, count):
        if i < size:
            return None
        ahead = i < (size + count) // 2
        blocks = (i - size) // size + 1 if ahead else (count - 1 - i) // size + 1
        return gx < PEERS_X - blocks if ahead else gx >= blocks

    def masked(value, i, size, count, mask):
        row_in = inside_x(i, size, count)
        keep = mask if row_in is None else jnp.logical_and(mask, row_in)
        return jnp.where(keep, value, 0.0), keep

    def inside_y(shape, own, ahead):
        row = iota(shape, 0)
        after = jnp.logical_and(jnp.logical_and(row >= own, row < ahead), gy < PEERS_Y - 1)
        return jnp.logical_or(row < own, jnp.logical_or(after, jnp.logical_and(row >= ahead, gy > 0)))

    def couplings(rows, size, count, permit, mask, kx, ky, kz, wrap):
        values = {}
        for i in rows:
            values[i] = masked(permit[i], i, size, count, mask)[0]
        shape = values[rows[0]].shape
        top = iota(shape, 1) == shape[1] - 1
        for i in rows:
            e = values[i]
            ky[i] = e + roll(e, -1, 0)
            along = e + roll(e, -1, 1)
            kz[i] = jnp.where(top, 0.0, along) if wrap else along
            after = (i + 1) % count
            if after in values:
                kx[i] = e + values[after]
        return values

    def diagonal(i, count, e, kx, ky, kz, wrap):
        y, z = ky[i], kz[i]
        total = kx[i] + kx[(i - 1) % count] + (y + roll(y, 1, 0)) + (z + roll(z, 1, 1))
        if wrap:
            lane = iota(e.shape, 1)
            ends = jnp.logical_or(lane == 0, lane == e.shape[1] - 1)
            total = total + jnp.where(ends, e, 0.0)
        return total

    def around(u, i, count, kx, ky, kz):
        here, y, z = u[i], ky[i], kz[i]
        before = (i - 1) % count
        total = kx[i] * u[(i + 1) % count] + kx[before] * u[before]
        total = total + (y * roll(here, -1, 0) + roll(y * here, 1, 0))
        return total + (z * roll(here, -1, 1) + roll(z * here, 1, 1))

    def reach(size, count, width):
        return list(range(size + width)) + list(range(count - width, count))

    hear(1)
    tell(2)

    z_in, z_out = iota((128, 128), 0), iota((128, 128), 1)
    pack_low = jnp.where(z_out == z_in // 2, 1.0, 0.0).astype(F32)
    pack_high = jnp.where(z_out == z_in // 2 + 64, 1.0, 0.0).astype(F32)

    def coarsen2(first, second):
        both = first + second
        low, high = both[0:1] + both[1:2], both[2:3] + both[3:4]
        return mix(low, pack_low) + mix(high, pack_high)

    copies["perm1"][NEAR.index((0, 0, 1))].wait_recv()
    near1 = [permit1[i, pl.ds(0, 8), :] for i in range(4)]
    stage3[0] = mix(jnp.concatenate([near1[0] + near1[1], near1[2] + near1[3]], axis=0), half_256)
    own2 = [stage3[0, pl.ds(8 * i, 4, stride=2), :] + stage3[0, pl.ds(8 * i + 1, 4, stride=2), :] for i in range(2)]
    perm_col[gx] = 0.015625 * coarsen2(own2[0], own2[1])

    arrive("perm0")
    lane0 = iota((24, 384), 1)
    beside = jnp.where(gz == 0, 1, 0)
    mask_z = jnp.logical_or(
        lane0 < 256,
        jnp.logical_or(jnp.logical_and(lane0 < 320, beside == 1), jnp.logical_and(lane0 >= 320, beside == 0)),
    )
    mask0 = jnp.logical_and(inside_y((24, 384), 16, 20), mask_z)
    e0 = couplings(reach(8, 16, 3), 8, 16, permit0, mask0, kx0, ky0, kz0, False)

    def diagonal0(i, e):
        keep = masked(e, i, 8, 16, mask0)[1]
        inv0[i] = jnp.where(keep, 1.0 / diagonal(i, 16, e, kx0, ky0, kz0, False), 0.0)

    def first0(i, charge):
        half0[i] = (2.0 * charge) * inv0[i]

    def second0(i):
        black0[i] = half0[i] + around(half0, i, 16, kx0, ky0, kz0) * inv0[i]

    for i in reach(8, 16, 2):
        diagonal0(i, e0[i])
    arrive("charge0")
    for i in reach(8, 16, 2):
        first0(i, charge0[i])
    for i in reach(8, 16, 1):
        second0(i)
    odd0 = (iota((16, 256), 0) + iota((16, 256), 1)) % 2
    left0 = []
    for i in range(8):
        rest = around(black0, i, 16, kx0, ky0, kz0)[:16, :256]
        left0.append(jnp.where(odd0 == i % 2, rest, 0.0))
    right1[pl.ds(0, 4), pl.ds(0, 8), lane_half] = 0.5 * coarsen0(left0)
    send1("right1", right1, 6, WIDE)
    hear(2)
    for i, o in enumerate(RING):
        send("perm3z", i, perm_col.at[gx], perm_col.at[gx], o)

    arrive("perm1", NEAR.index((0, 0, 1)))
    mask1 = inside_y((24, 256), 8, 16)
    e1 = couplings(range(18), 4, 18, permit1, mask1, kx1, ky1, kz1, True)

    def coarsen1(rows, ref, cells):
        half = len(rows) // 2
        pairs = [rows[2 * i] + rows[2 * i + 1] for i in range(half)]
        stage1[pl.ds(0, half)] = mix(jnp.concatenate(pairs, axis=0), half_256).reshape(half, 24, 128)
        for j, cell in enumerate(cells):
            ref[cell, pl.ds(0, 8), :] = stage1[j, pl.ds(0, 8, stride=2), :] + stage1[j, pl.ds(1, 8, stride=2), :]
            ref[cell, pl.ds(12, 4), :] = stage1[j, pl.ds(16, 4, stride=2), :] + stage1[j, pl.ds(17, 4, stride=2), :]

    cells2 = (0, 1, 2, 3, 4, 7, 8, 9)
    coarsen1([0.125 * e1[i] for i in (0, 1, 2, 3, 4, 5, 6, 7, 8, 9, 12, 13, 14, 15, 16, 17)], stage2, cells2)
    mask2 = inside_y((16, 128), 4, 8)
    e2 = couplings(cells2, 2, 10, stage2, mask2, kx2, ky2, kz2, True)
    inverse2 = {}
    for i in reach(2, 10, 2):
        keep = masked(e2[i], i, 2, 10, mask2)[1]
        inverse2[i] = jnp.where(keep, 1.0 / diagonal(i, 10, e2[i], kx2, ky2, kz2, True), 0.0)
    for i in range(2):
        permit2[0, i, pl.ds(0, 4), :] = e2[i][:4]
        permit2[1, i, pl.ds(0, 4), :] = inverse2[i][:4]

    def span_far(step):
        if step == 0:
            return pl.ds(0, 2), pl.ds(0, 2)
        start = {1: 8, 2: 6, -1: 2, -2: 4}[step]
        return pl.ds(0, 2), pl.ds(start, 2)

    whole_q = pl.ds(0, 2)
    for i, o in enumerate(FAR):
        (sx, dx), (sy, dy) = span_far(o[0]), span(o[1], 4, 16, 4)
        send("perm2", i, permit2.at[whole_q, sx, sy], permit2.at[whole_q, dx, dy], o)
    for i in reach(4, 18, 6):
        keep = masked(e1[i], i, 4, 18, mask1)[1]
        inv1[i] = jnp.where(keep, 1.0 / diagonal(i, 18, e1[i], kx1, ky1, kz1, True), 0.0)

    arrive("perm0far")
    arrive("charge0far")
    edge = jnp.logical_or(iota((24, 384), 0) >= 16, lane0 >= 256)
    far_permit = {i: permit0[i] for i in range(8, 16)}
    far_permit[10] = jnp.where(edge, edge_permit[0], far_permit[10])
    far_permit[13] = jnp.where(edge, edge_permit[1], far_permit[13])
    far_charge = {i: charge0[i] for i in (8, 9, 10, 13, 14, 15)}
    far_charge[9] = jnp.where(edge, edge_charge[0], far_charge[9])
    far_charge[14] = jnp.where(edge, edge_charge[1], far_charge[14])
    e0 = couplings(range(8, 16), 8, 16, far_permit, mask0, kx0, ky0, kz0, False)
    for i in (8, 9, 10, 13, 14, 15):
        diagonal0(i, e0[i])
    for i in (8, 9, 10, 13, 14, 15):
        first0(i, far_charge[i])
    for i in (8, 9, 14, 15):
        second0(i)

    arrive("right1")
    for i in reach(4, 18, 6):
        half1[i] = right1[i] * inv1[i]
    for i in reach(4, 18, 5):
        black1[i] = half1[i] + around(half1, i, 18, kx1, ky1, kz1) * inv1[i]
    odd1 = (iota((24, 256), 0) + iota((24, 256), 1)) % 2
    left1 = []
    for i in reach(4, 18, 4):
        left1.append(jnp.where(odd1 == i % 2, 0.5 * around(black1, i, 18, kx1, ky1, kz1), 0.0))
    coarsen1(left1, right2, (0, 1, 2, 3, 8, 9))

    for i in reach(2, 10, 2):
        half2[i] = right2[i] * inverse2[i]
    for i in reach(2, 10, 1):
        black2[i] = half2[i] + around(half2, i, 10, kx2, ky2, kz2) * inverse2[i]
    odd2 = (iota((4, 128), 0) + iota((4, 128), 1)) % 2
    left2 = []
    for i in range(2):
        rest = around(black2, i, 10, kx2, ky2, kz2)[:4]
        left2.append(jnp.where(odd2 == i % 2, rest, 0.0))
    right_col[gx] = 0.5 * coarsen2(left2[0], left2[1])
    for i, o in enumerate(RING):
        send("right3z", i, right_col.at[gx], right_col.at[gx], o)
    for i in range(2):
        late2[0, i, pl.ds(0, 4), :] = right2[i, :4]
        late2[1, i, pl.ds(0, 4), :] = black2[i, :4]
    for i, o in enumerate(FAR):
        (sx, dx), (sy, dy) = span_far(o[0]), span(o[1], 4, 16, 4)
        send("late2", i, late2.at[whole_q, sx, sy], late2.at[whole_q, dx, dy], o)

    arrive("perm3z")
    perm_all[gy] = perm_col[...].reshape(16, 128)
    for i, o in enumerate(PLANE):
        send("perm3y", i, perm_all.at[gy], perm_all.at[gy], o)
    arrive("perm2")
    couplings(range(10), 2, 10, permit2.at[0], mask2, kx2, ky2, kz2, True)
    for i in reach(2, 10, 3):
        inverse2[i] = masked(permit2[1, i], i, 2, 10, mask2)[0]

    arrive("perm3y")

    def ahead(u):
        return jnp.concatenate([u[1:], u[:1]], axis=0)

    def behind(u):
        return jnp.concatenate([u[-1:], u[:-1]], axis=0)

    def steps_of(extent_y, extent_x, extent_z, shape):
        y, x, z = iota(shape, 0), iota(shape, 1), iota(shape, 2)
        return [
            (ahead, y < extent_y - 1), (behind, y > 0),
            (lambda u: roll(u, -1, 1), x < extent_x - 1), (lambda u: roll(u, 1, 1), x > 0),
            (lambda u: roll(u, -1, 2), z < extent_z - 1), (lambda u: roll(u, 1, 2), z > 0),
        ]

    shape3 = (16, 16, 128)
    pair3, x3, lane3 = iota(shape3, 0), iota(shape3, 1), iota(shape3, 2)
    upper3 = lane3 >= 64
    z3 = lane3 % 64

    def across(u):
        turned = roll(u, 64, 2)
        return jnp.where(upper3, ahead(turned), behind(turned))

    steps3 = [
        (lambda u: roll(u, 64, 2), None),
        (across, jnp.logical_or(jnp.logical_and(upper3, pair3 < 15), jnp.logical_and(lane3 < 64, pair3 > 0))),
        (lambda u: roll(u, -1, 1), x3 < 15), (lambda u: roll(u, 1, 1), x3 > 0),
        (lambda u: roll(u, -1, 2), z3 < 63), (lambda u: roll(u, 1, 2), z3 > 0),
    ]

    def prepare(e, steps, cells):
        couple, total = [], None
        for shift, there in steps:
            k = e + shift(e)
            term = k if there is None else jnp.where(there, k, e)
            couple.append(k if there is None else jnp.where(there, k, 0.0))
            total = term if total is None else total + term
        inverse = 1.0 / total if cells is None else jnp.where(cells, 1.0 / total, 0.0)
        return couple, inverse

    def sum_around(u, steps, couple):
        total = None
        for (shift, _), k in zip(steps, couple):
            total = k * shift(u) if total is None else total + k * shift(u)
        return total

    pack3 = jnp.where(z_out == (z_in % 64) // 2, 1.0, 0.0).astype(F32)
    pack4 = jnp.where(z_out == z_in // 2, 1.0, 0.0).astype(F32)
    spread4 = jnp.where(jnp.logical_and(z_in == (z_out % 64) // 2, z_in < 32), 1.0, 0.0).astype(F32)
    spread5 = jnp.where(jnp.logical_and(z_in == z_out // 2, z_in < 16), 1.0, 0.0).astype(F32)

    def coarsen3(u):
        stage3[...] = mix(u.reshape(256, 128), pack3).reshape(16, 16, 128)
        return stage3[:, pl.ds(0, 8, stride=2), :] + stage3[:, pl.ds(1, 8, stride=2), :]

    def coarsen4(u):
        pairs = jnp.concatenate([u[2 * i : 2 * i + 1] + u[2 * i + 1 : 2 * i + 2] for i in range(8)], axis=0)
        stage4[...] = mix(pairs.reshape(64, 128), pack4).reshape(8, 8, 128)
        stage5[...] = jnp.zeros_like(stage5)
        stage5[:, pl.ds(0, 4), :] = stage4[:, pl.ds(0, 4, stride=2), :] + stage4[:, pl.ds(1, 4, stride=2), :]
        return stage5[...]

    shape4, shape5 = (16, 8, 128), (8, 8, 128)
    steps4, steps5 = steps_of(16, 8, 32, shape4), steps_of(8, 4, 16, shape5)
    e3 = perm_all[...]
    k3, inverse3 = prepare(e3, steps3, None)
    for j in range(6):
        couple3[j] = k3[j]
    couple3[6] = inverse3
    e4 = 0.125 * coarsen3(e3)
    k4, inverse4 = prepare(e4, steps4, iota(shape4, 2) < 32)
    e5 = 0.125 * coarsen4(e4)
    k5, inverse5 = prepare(e5, steps5, jnp.logical_and(iota(shape5, 2) < 16, iota(shape5, 1) < 4))
    even3 = (x3 + z3 + lane3 // 64) % 2 == 0
    even4 = (iota(shape4, 0) + iota(shape4, 1) + iota(shape4, 2)) % 2 == 0
    even5 = (iota(shape5, 0) + iota(shape5, 1) + iota(shape5, 2)) % 2 == 0

    arrive("right3z")
    right_all[gy] = right_col[...].reshape(16, 128)
    for i, o in enumerate(PLANE):
        send("right3y", i, right_all.at[gy], right_all.at[gy], o)
    arrive("late2")
    arrive("right3y")

    g3 = right_all[...]
    first3 = g3 * inverse3
    dark3 = (g3 + sum_around(first3, steps3, k3)) * inverse3
    rest3 = sum_around(dark3, steps3, k3)
    g4 = 0.5 * coarsen3(jnp.where(even3, rest3, 0.0))
    first4 = g4 * inverse4
    dark4 = (g4 + sum_around(first4, steps4, k4)) * inverse4
    rest4 = sum_around(dark4, steps4, k4)
    g5 = 0.5 * coarsen4(jnp.where(even4, rest4, 0.0))
    light5 = g5 * inverse5
    dark5 = (g5 + sum_around(light5, steps5, k5)) * inverse5
    for _ in range(3):
        light5 = (g5 + sum_around(dark5, steps5, k5)) * inverse5
        dark5 = (g5 + sum_around(light5, steps5, k5)) * inverse5
    u5 = jnp.where(even5, light5, dark5)
    wide5 = mix(u5.reshape(64, 128), spread5).reshape(8, 8, 128)[:, :4]
    stage4[:, pl.ds(0, 4, stride=2), :] = wide5
    stage4[:, pl.ds(1, 4, stride=2), :] = wide5
    c4 = jnp.concatenate([stage4[i // 2 : i // 2 + 1] for i in range(16)], axis=0)
    light4 = (g4 + sum_around(dark4 + c4, steps4, k4)) * inverse4
    end4 = (g4 + sum_around(light4, steps4, k4)) * inverse4
    u4 = jnp.where(even4, light4, end4)
    up4[...] = u4

    def plane_of(step):
        return lax.rem(gy + (step + PEERS_Y), PEERS_Y)

    near4 = mix(jnp.concatenate([up4[plane_of(p)] for p in range(-3, 5)], axis=0), spread4).reshape(8, 8, 128)
    stage3[pl.ds(0, 8), pl.ds(0, 8, stride=2), :] = near4
    stage3[pl.ds(0, 8), pl.ds(1, 8, stride=2), :] = near4
    up3[...] = g3 + rest3
    upper_plane = iota((16, 128), 1) >= 64
    even_plane = (iota((16, 128), 0) + iota((16, 128), 1) + iota((16, 128), 1) // 64) % 2 == 0

    def around3(u, p):
        at = plane_of(p)
        here = u[p]
        beyond = jnp.where(upper_plane, roll(u[p + 1], 64, 1), roll(u[p - 1], 64, 1))
        total = couple3[0, at] * roll(here, 64, 1) + couple3[1, at] * beyond
        total = total + (couple3[2, at] * roll(here, -1, 0) + couple3[3, at] * roll(here, 1, 0))
        return total + (couple3[4, at] * roll(here, -1, 1) + couple3[5, at] * roll(here, 1, 1))

    corr3 = {p: stage3[p + 3] for p in range(-3, 4)}
    light3 = {p: (up3[plane_of(p)] + around3(corr3, p)) * couple3[6, plane_of(p)] for p in range(-2, 3)}
    end3 = {}
    for p in range(-1, 2):
        dark = (right_all[plane_of(p)] + around3(light3, p)) * couple3[6, plane_of(p)]
        end3[p] = jnp.where(even_plane, light3[p], dark)

    spread3 = jnp.concatenate(
        [
            jnp.where(z_in == z_out // 2, 1.0, 0.0).astype(F32),
            jnp.where(z_in == z_out // 2 + 64, 1.0, 0.0).astype(F32),
        ],
        axis=1,
    )
    for dy, base in ((0, 0), (1, 4), (-1, 12)):
        turned = pltpu.roll(end3[dy], lax.rem(PEERS_X - gx, PEERS_X), 0)
        wide = mix(turned, spread3)
        for cell, row in ((0, 0), (1, 2), (2, 4), (14, 6), (15, 8)):
            low = jnp.broadcast_to(wide[cell : cell + 1, :128], (2, 128))
            high = jnp.broadcast_to(wide[cell : cell + 1, 128:], (2, 128))
            for i in (row, row + 1):
                stage2[i, pl.ds(base, 2), :] = low
                stage2[i, pl.ds(base + 2, 2), :] = high
    for i in range(10):
        half2[i] = masked(late2[1, i] + stage2[i], i, 2, 10, mask2)[0]
    for i in reach(2, 10, 3):
        red2[i] = (late2[0, i] + around(half2, i, 10, kx2, ky2, kz2)) * inverse2[i]
    even2 = (iota((16, 128), 0) + iota((16, 128), 1)) % 2
    u2 = {}
    for i in reach(2, 10, 2):
        dark = (late2[0, i] + around(red2, i, 10, kx2, ky2, kz2)) * inverse2[i]
        u2[i] = jnp.where(even2 == i % 2, red2[i], dark)

    spread2 = jnp.where(iota((128, 256), 0) == iota((128, 256), 1) // 2, 1.0, 0.0).astype(F32)
    order2 = (0, 1, 2, 3, 8, 9)
    for j, cell in enumerate(order2):
        plane = u2[cell]
        stage1[j, pl.ds(0, 4, stride=2), :] = plane[:4]
        stage1[j, pl.ds(1, 4, stride=2), :] = plane[:4]
        for row, source in ((8, 4), (10, 5), (20, 14), (22, 15)):
            stage1[j, pl.ds(row, 2), :] = jnp.broadcast_to(plane[source : source + 1], (2, 128))
    wide2 = mix(stage1[pl.ds(0, 6)].reshape(144, 128), spread2)
    for j, cell in enumerate(order2):
        for i in {0: (0, 1), 1: (2, 3), 2: (4, 5), 3: (6,), 8: (15,), 9: (16, 17)}[cell]:
            part = black1[i] + wide2[24 * j : 24 * j + 24]
            half1[i] = masked(part, i, 4, 18, mask1)[0]
    for i in reach(4, 18, 2):
        red1[i] = (right1[i] + around(half1, i, 18, kx1, ky1, kz1)) * inv1[i]
    u1 = {}
    for i in reach(4, 18, 1):
        dark = (right1[i] + around(red1, i, 18, kx1, ky1, kz1)) * inv1[i]
        u1[i] = jnp.where(odd1 == i % 2, red1[i], dark)

    order1 = (0, 1, 2, 3, 4, 17)
    halo_lane = jnp.where(z_out < 64, z_out // 2, 64 + z_out // 2)
    spread_halo = jnp.where(z_in == halo_lane, 1.0, 0.0).astype(F32)
    for j, cell in enumerate(order1):
        low, high = u1[cell][:, :128], u1[cell][:, 128:]
        for part, plane in ((0, jnp.where(beside == 1, low, high)), (1, jnp.where(beside == 1, high, low))):
            stage6[part, j, pl.ds(0, 8, stride=2), :] = plane[:8]
            stage6[part, j, pl.ds(1, 8, stride=2), :] = plane[:8]
            stage6[part, j, pl.ds(16, 2), :] = jnp.broadcast_to(plane[8:9], (2, 128))
            stage6[part, j, pl.ds(22, 2), :] = jnp.broadcast_to(plane[23:24], (2, 128))
    wide1 = mix(stage6[0].reshape(144, 128), spread2)
    edge1 = mix(stage6[1].reshape(144, 128), spread_halo)
    for j, cell in enumerate(order1):
        for i in {0: (0, 1), 1: (2, 3), 2: (4, 5), 3: (6, 7), 4: (8, 9), 17: (14, 15)}[cell]:
            part = jnp.concatenate([wide1[24 * j : 24 * j + 24], edge1[24 * j : 24 * j + 24]], axis=1)
            half0[i] = masked(black0[i] + part, i, 8, 16, mask0)[0]
    for i in reach(8, 16, 1):
        red0[i] = (2.0 * charge0[i] + around(half0, i, 16, kx0, ky0, kz0)) * inv0[i]
    for i in range(8):
        dark = (2.0 * charge0[i] + around(red0, i, 16, kx0, ky0, kz0)) * inv0[i]
        out_ref[i] = jnp.where(odd0 == i % 2, red0[i, :16, :256], dark[:16, :256])

    for group in copies.values():
        for copy in group:
            copy.wait_send()


def per_device(charge, permittivity):
    def vmem(*shape):
        return pltpu.VMEM(shape, F32)

    fine, middle, coarse = (16, 24, 384), (18, 24, 256), (10, 16, 128)
    scratch = [vmem(*fine) for _ in range(9)] + [vmem(4, 16, 128), vmem(2, 24, 384), vmem(2, 24, 384)]
    scratch += [vmem(*middle) for _ in range(9)] + [vmem(8, 24, 128)]
    scratch += [vmem(2, *coarse)] + [vmem(*coarse) for _ in range(7)] + [vmem(2, *coarse), vmem(*coarse)]
    scratch += [vmem(16, 1, 128), vmem(16, 16, 128), vmem(16, 1, 128), vmem(16, 16, 128)]
    scratch += [vmem(16, 16, 128), vmem(8, 8, 128), vmem(8, 8, 128), vmem(2, 6, 24, 128)]
    scratch += [vmem(7, 16, 16, 128), vmem(16, 16, 128), vmem(16, 8, 128)]
    scratch += [pltpu.SemaphoreType.DMA((2,)), pltpu.SemaphoreType.DMA((TOTAL,)), pltpu.SemaphoreType.DMA((TOTAL,))]
    scratch += [pltpu.SemaphoreType.REGULAR((3,))]
    return pl.pallas_call(
        kernel,
        out_shape=jax.ShapeDtypeStruct(charge.shape, F32),
        in_specs=[pl.BlockSpec(memory_space=pl.ANY)] * 2,
        out_specs=pl.BlockSpec(memory_space=pltpu.VMEM),
        scratch_shapes=scratch,
        compiler_params=pltpu.CompilerParams(
            collective_id=0, has_side_effects=True, vmem_limit_bytes=55040 * 1024
        ),
        name="vcycle",
    )(charge, permittivity)


def solution(mesh):
    return jax.shard_map(
        per_device,
        mesh=mesh,
        in_specs=(P("gx", "gy", "gz"), P("gx", "gy", "gz")),
        out_specs=P("gx", "gy", "gz"),
        check_vma=False,
    )
```

```python
import jax
import jax.numpy as jnp
from jax import lax
from jax.experimental import pallas as pl
from jax.experimental.pallas import tpu as pltpu
from jax.sharding import PartitionSpec as P

MESH = pl.DeviceIdType.MESH
F32 = jnp.float32
PEERS_X = 16
PEERS_Y = 16

NEAR = [(a, b, c) for c in (0, 1) for a in (-1, 0, 1) for b in (-1, 0, 1) if (a, b, c) != (0, 0, 0)]
NEAR.sort(key=lambda o: (-abs(o[0]), -sum(abs(step) for step in o)))
SAME = [o for o in NEAR if o[2] == 0]
FAR = SAME + [(a, b, 0) for a in (-2, 2) for b in (-1, 0, 1)]
WIDE = NEAR + [(a, b, c) for c in (0, 1) for a in (-2, 2) for b in (-1, 0, 1)]
SIDE = [o for o in NEAR if o[0]]
RING = [(i, 0, 0) for i in sorted(range(-7, 9), key=lambda i: -abs(i)) if i]
PLANE = [(0, i, 0) for i in (6, -6, 2, -2, 5, 7, -5, -7, 8, 3, -3, 4, -4, 1, -1)]

COUNTS = {
    "charge0": len(NEAR), "perm0": len(NEAR), "charge0far": len(SIDE), "perm0far": len(SIDE), "perm1": len(WIDE),
    "right1": len(WIDE), "perm2": len(FAR), "perm3z": len(RING), "perm3y": len(PLANE), "right3z": len(RING),
    "right3y": len(PLANE), "late2": len(FAR),
}
BASE = {}
TOTAL = 0
for _key, _count in COUNTS.items():
    BASE[_key] = TOTAL
    TOTAL += _count


def iota(shape, dim):
    return lax.broadcasted_iota(jnp.int32, shape, dim)


def roll(value, shift, axis):
    return pltpu.roll(value, shift % value.shape[axis], axis)


def mix(left, right):
    if left.shape[0] % 16:
        return jnp.dot(left, right, precision=lax.Precision.HIGHEST, preferred_element_type=F32)
    ones, total = right.astype(jnp.bfloat16), None
    for _ in range(3):
        part = left.astype(jnp.bfloat16)
        left = left - part.astype(F32)
        term = jnp.dot(part, ones, preferred_element_type=F32)
        total = term if total is None else total + term
    return total


def halver(size, out):
    return jnp.where(iota((size, out), 0) // 2 == iota((size, out), 1), 1.0, 0.0).astype(F32)


def span(step, size, count, width):
    if step == 0:
        return pl.ds(0, size), pl.ds(0, size)
    if step > 0:
        return pl.ds(size - width, width), pl.ds(count - width, width)
    return pl.ds(0, width), pl.ds(size, width)


def kernel(
    charge_hbm, permit_hbm, out_ref,
    charge0, permit0, kx0, ky0, kz0, inv0, half0, black0, red0, stage0, edge_permit, edge_charge,
    permit1, kx1, ky1, kz1, inv1, right1, half1, black1, red1, stage1,
    permit2, kx2, ky2, kz2, right2, half2, black2, red2, late2, stage2,
    perm_col, perm_all, right_col, right_all, stage3, stage4, stage5, stage6, couple3, up3, up4,
    local_sem, send_sem, recv_sem, token_sem,
):
    gx, gy, gz = lax.axis_index("gx"), lax.axis_index("gy"), lax.axis_index("gz")

    def peer(o):
        return (
            lax.rem(gx + (o[0] + PEERS_X), PEERS_X),
            lax.rem(gy + (o[1] + PEERS_Y), PEERS_Y),
            (1 - gz) if o[2] else gz,
        )

    copies = {}

    def send(name, index, src, dst, o):
        slot = BASE[name] + index
        copy = pltpu.make_async_remote_copy(
            src_ref=src, dst_ref=dst, send_sem=send_sem.at[slot], recv_sem=recv_sem.at[slot],
            device_id=peer(o), device_id_type=MESH,
        )
        copy.start()
        copies.setdefault(name, []).append(copy)

    def arrive(name, skip=None):
        for index, copy in enumerate(copies[name]):
            if index != skip:
                copy.wait_recv()

    barrier = pltpu.get_barrier_semaphore()
    for o in NEAR:
        pl.semaphore_signal(barrier, inc=1, device_id=peer(o), device_id_type=MESH)
    own0 = (pl.ds(0, 8), pl.ds(0, 16), pl.ds(0, 256))
    fetch_permit = pltpu.make_async_copy(permit_hbm, permit0.at[own0], local_sem.at[0])
    fetch_charge = pltpu.make_async_copy(charge_hbm, charge0.at[own0], local_sem.at[1])
    fetch_permit.start()
    fetch_charge.start()
    half_256 = halver(256, 128)
    lane_half = pl.ds(pl.multiple_of(gz * 128, 128), 128)

    def coarsen0(rows):
        pairs = [rows[2 * i] + rows[2 * i + 1] for i in range(4)]
        stage0[...] = mix(jnp.concatenate(pairs, axis=0), half_256).reshape(4, 16, 128)
        return stage0[:, pl.ds(0, 8, stride=2), :] + stage0[:, pl.ds(1, 8, stride=2), :]

    def tell(turn):
        step = 2**turn
        for o in ((step, 0, 0), (-step, 0, 0), (0, step, 0), (0, -step, 0)):
            pl.semaphore_signal(token_sem.at[turn], inc=1, device_id=peer(o), device_id_type=MESH)

    def hear(turn):
        pl.semaphore_wait(token_sem.at[turn], 4)

    def send0(name, source, ref, reach, far):
        for i, o in enumerate(SIDE if far else NEAR):
            away = sum(abs(step) for step in o)
            width = reach + 1 - away
            sx, dx, target = pl.ds(0, 8), pl.ds(0, 8), ref
            if far and away == 3:
                continue
            if o[0]:
                last = 1 if away < 3 else 0
                rows = 1 if far else width - last
                start = (width - 1 if far else 0) if o[0] < 0 else 8 - (width if far else width - last)
                sx, dx = pl.ds(start, rows), pl.ds(start + 8, rows)
                if far and away == 2:
                    target, dx = (edge_permit if reach == 4 else edge_charge), pl.ds(0 if o[0] < 0 else 1, 1)
            sy, dy = span(o[1], 16, 24, width)
            if o[2]:
                sz, dz = pl.ds(pl.multiple_of((1 - gz) * 128, 128), 128), pl.ds(256, 128)
            else:
                sz, dz = pl.ds(0, 256), pl.ds(0, 256)
            send(name, i, source.at[sx, sy, sz], target.at[dx, dy, dz], o)

    pl.semaphore_wait(barrier, len(NEAR))
    tell(0)
    send0("perm0", permit_hbm, permit0, 4, False)
    send0("charge0", charge_hbm, charge0, 3, False)

    fetch_permit.wait()
    permit1[pl.ds(0, 4), pl.ds(0, 8), lane_half] = 0.125 * coarsen0([permit0[i, :16, :256] for i in range(8)])
    fetch_charge.wait()

    def send1(name, ref, reach, peers):
        for i, o in sorted(enumerate(WIDE), key=lambda pair: -abs(pair[1][0])):
            if o not in peers:
                continue
            away = abs(o[0])
            along = {0: 4, 1: 4, 2: reach - 4 - abs(o[1])}[away]
            across = {0: reach, 1: reach - 1, 2: reach - 5}[away]
            if away < 2:
                sx, dx = span(o[0], 4, 18, along)
            else:
                sx = pl.ds(4 - along, along) if o[0] > 0 else pl.ds(0, along)
                dx = pl.ds(14 - along, along) if o[0] > 0 else pl.ds(8, along)
            sy, dy = span(o[1], 8, 24, across)
            send(name, i, ref.at[sx, sy, lane_half], ref.at[dx, dy, lane_half], o)

    send1("perm1", permit1, 7, NEAR)
    hear(0)
    tell(1)
    send1("perm1", permit1, 7, WIDE[len(NEAR):])
    send0("perm0far", permit_hbm, permit0, 4, True)
    send0("charge0far", charge_hbm, charge0, 3, True)

    def inside_x(i, size, count):
        if i < size:
            return None
        ahead = i < (size + count) // 2
        blocks = (i - size) // size + 1 if ahead else (count - 1 - i) // size + 1
        return gx < PEERS_X - blocks if ahead else gx >= blocks

    def masked(value, i, size, count, mask):
        row_in = inside_x(i, size, count)
        keep = mask if row_in is None else jnp.logical_and(mask, row_in)
        return jnp.where(keep, value, 0.0), keep

    def inside_y(shape, own, ahead):
        row = iota(shape, 0)
        after = jnp.logical_and(jnp.logical_and(row >= own, row < ahead), gy < PEERS_Y - 1)
        return jnp.logical_or(row < own, jnp.logical_or(after, jnp.logical_and(row >= ahead, gy > 0)))

    def couplings(rows, size, count, permit, mask, kx, ky, kz, wrap):
        values = {}
        for i in rows:
            values[i] = masked(permit[i], i, size, count, mask)[0]
        shape = values[rows[0]].shape
        top = iota(shape, 1) == shape[1] - 1
        for i in rows:
            e = values[i]
            ky[i] = e + roll(e, -1, 0)
            along = e + roll(e, -1, 1)
            kz[i] = jnp.where(top, 0.0, along) if wrap else along
            after = (i + 1) % count
            if after in values:
                kx[i] = e + values[after]
        return values

    def diagonal(i, count, e, kx, ky, kz, wrap):
        y, z = ky[i], kz[i]
        total = kx[i] + kx[(i - 1) % count] + (y + roll(y, 1, 0)) + (z + roll(z, 1, 1))
        if wrap:
            lane = iota(e.shape, 1)
            ends = jnp.logical_or(lane == 0, lane == e.shape[1] - 1)
            total = total + jnp.where(ends, e, 0.0)
        return total

    def around(u, i, count, kx, ky, kz):
        here, y, z = u[i], ky[i], kz[i]
        before = (i - 1) % count
        total = kx[i] * u[(i + 1) % count] + kx[before] * u[before]
        total = total + (y * roll(here, -1, 0) + roll(y * here, 1, 0))
        return total + (z * roll(here, -1, 1) + roll(z * here, 1, 1))

    def reach(size, count, width):
        return list(range(size + width)) + list(range(count - width, count))

    hear(1)
    tell(2)

    z_in, z_out = iota((128, 128), 0), iota((128, 128), 1)
    pack_low = jnp.where(z_out == z_in // 2, 1.0, 0.0).astype(F32)
    pack_high = jnp.where(z_out == z_in // 2 + 64, 1.0, 0.0).astype(F32)

    def coarsen2(first, second):
        both = first + second
        low, high = both[0:1] + both[1:2], both[2:3] + both[3:4]
        return mix(low, pack_low) + mix(high, pack_high)

    copies["perm1"][NEAR.index((0, 0, 1))].wait_recv()
    near1 = [permit1[i, pl.ds(0, 8), :] for i in range(4)]
    stage3[0] = mix(jnp.concatenate([near1[0] + near1[1], near1[2] + near1[3]], axis=0), half_256)
    own2 = [stage3[0, pl.ds(8 * i, 4, stride=2), :] + stage3[0, pl.ds(8 * i + 1, 4, stride=2), :] for i in range(2)]
    perm_col[gx] = 0.015625 * coarsen2(own2[0], own2[1])

    arrive("perm0")
    lane0 = iota((24, 384), 1)
    beside = jnp.where(gz == 0, 1, 0)
    mask_z = jnp.logical_or(
        lane0 < 256,
        jnp.logical_or(jnp.logical_and(lane0 < 320, beside == 1), jnp.logical_and(lane0 >= 320, beside == 0)),
    )
    mask0 = jnp.logical_and(inside_y((24, 384), 16, 20), mask_z)
    e0 = couplings(reach(8, 16, 3), 8, 16, permit0, mask0, kx0, ky0, kz0, False)

    def diagonal0(i, e):
        keep = masked(e, i, 8, 16, mask0)[1]
        inv0[i] = jnp.where(keep, 1.0 / diagonal(i, 16, e, kx0, ky0, kz0, False), 0.0)

    def first0(i, charge):
        half0[i] = (2.0 * charge) * inv0[i]

    def second0(i):
        black0[i] = half0[i] + around(half0, i, 16, kx0, ky0, kz0) * inv0[i]

    for i in reach(8, 16, 2):
        diagonal0(i, e0[i])
    arrive("charge0")
    for i in reach(8, 16, 2):
        first0(i, charge0[i])
    for i in reach(8, 16, 1):
        second0(i)
    odd0 = (iota((16, 256), 0) + iota((16, 256), 1)) % 2
    left0 = []
    for i in range(8):
        rest = around(black0, i, 16, kx0, ky0, kz0)[:16, :256]
        left0.append(jnp.where(odd0 == i % 2, rest, 0.0))
    right1[pl.ds(0, 4), pl.ds(0, 8), lane_half] = 0.5 * coarsen0(left0)
    send1("right1", right1, 6, WIDE)
    hear(2)
    for i, o in enumerate(RING):
        send("perm3z", i, perm_col.at[gx], perm_col.at[gx], o)

    arrive("perm1", NEAR.index((0, 0, 1)))
    mask1 = inside_y((24, 256), 8, 16)
    e1 = couplings(range(18), 4, 18, permit1, mask1, kx1, ky1, kz1, True)

    def coarsen1(rows, ref, cells):
        half = len(rows) // 2
        pairs = [rows[2 * i] + rows[2 * i + 1] for i in range(half)]
        stage1[pl.ds(0, half)] = mix(jnp.concatenate(pairs, axis=0), half_256).reshape(half, 24, 128)
        for j, cell in enumerate(cells):
            ref[cell, pl.ds(0, 8), :] = stage1[j, pl.ds(0, 8, stride=2), :] + stage1[j, pl.ds(1, 8, stride=2), :]
            ref[cell, pl.ds(12, 4), :] = stage1[j, pl.ds(16, 4, stride=2), :] + stage1[j, pl.ds(17, 4, stride=2), :]

    cells2 = (0, 1, 2, 3, 4, 7, 8, 9)
    coarsen1([0.125 * e1[i] for i in (0, 1, 2, 3, 4, 5, 6, 7, 8, 9, 12, 13, 14, 15, 16, 17)], stage2, cells2)
    mask2 = inside_y((16, 128), 4, 8)
    e2 = couplings(cells2, 2, 10, stage2, mask2, kx2, ky2, kz2, True)
    inverse2 = {}
    for i in reach(2, 10, 2):
        keep = masked(e2[i], i, 2, 10, mask2)[1]
        inverse2[i] = jnp.where(keep, 1.0 / diagonal(i, 10, e2[i], kx2, ky2, kz2, True), 0.0)
    for i in range(2):
        permit2[0, i, pl.ds(0, 4), :] = e2[i][:4]
        permit2[1, i, pl.ds(0, 4), :] = inverse2[i][:4]

    def span_far(step):
        if step == 0:
            return pl.ds(0, 2), pl.ds(0, 2)
        start = {1: 8, 2: 6, -1: 2, -2: 4}[step]
        return pl.ds(0, 2), pl.ds(start, 2)

    whole_q = pl.ds(0, 2)
    for i, o in enumerate(FAR):
        (sx, dx), (sy, dy) = span_far(o[0]), span(o[1], 4, 16, 4)
        send("perm2", i, permit2.at[whole_q, sx, sy], permit2.at[whole_q, dx, dy], o)
    for i in reach(4, 18, 6):
        keep = masked(e1[i], i, 4, 18, mask1)[1]
        inv1[i] = jnp.where(keep, 1.0 / diagonal(i, 18, e1[i], kx1, ky1, kz1, True), 0.0)

    arrive("perm0far")
    arrive("charge0far")
    edge = jnp.logical_or(iota((24, 384), 0) >= 16, lane0 >= 256)
    far_permit = {i: permit0[i] for i in range(8, 16)}
    far_permit[10] = jnp.where(edge, edge_permit[0], far_permit[10])
    far_permit[13] = jnp.where(edge, edge_permit[1], far_permit[13])
    far_charge = {i: charge0[i] for i in (8, 9, 10, 13, 14, 15)}
    far_charge[9] = jnp.where(edge, edge_charge[0], far_charge[9])
    far_charge[14] = jnp.where(edge, edge_charge[1], far_charge[14])
    e0 = couplings(range(8, 16), 8, 16, far_permit, mask0, kx0, ky0, kz0, False)
    for i in (8, 9, 10, 13, 14, 15):
        diagonal0(i, e0[i])
    for i in (8, 9, 10, 13, 14, 15):
        first0(i, far_charge[i])
    for i in (8, 9, 14, 15):
        second0(i)

    arrive("right1")
    for i in reach(4, 18, 6):
        half1[i] = right1[i] * inv1[i]
    for i in reach(4, 18, 5):
        black1[i] = half1[i] + around(half1, i, 18, kx1, ky1, kz1) * inv1[i]
    odd1 = (iota((24, 256), 0) + iota((24, 256), 1)) % 2
    left1 = []
    for i in reach(4, 18, 4):
        left1.append(jnp.where(odd1 == i % 2, 0.5 * around(black1, i, 18, kx1, ky1, kz1), 0.0))
    coarsen1(left1, right2, (0, 1, 2, 3, 8, 9))

    for i in reach(2, 10, 2):
        half2[i] = right2[i] * inverse2[i]
    for i in reach(2, 10, 1):
        black2[i] = half2[i] + around(half2, i, 10, kx2, ky2, kz2) * inverse2[i]
    odd2 = (iota((4, 128), 0) + iota((4, 128), 1)) % 2
    left2 = []
    for i in range(2):
        rest = around(black2, i, 10, kx2, ky2, kz2)[:4]
        left2.append(jnp.where(odd2 == i % 2, rest, 0.0))
    right_col[gx] = 0.5 * coarsen2(left2[0], left2[1])
    for i, o in enumerate(RING):
        send("right3z", i, right_col.at[gx], right_col.at[gx], o)
    for i in range(2):
        late2[0, i, pl.ds(0, 4), :] = right2[i, :4]
        late2[1, i, pl.ds(0, 4), :] = black2[i, :4]
    for i, o in enumerate(FAR):
        (sx, dx), (sy, dy) = span_far(o[0]), span(o[1], 4, 16, 4)
        send("late2", i, late2.at[whole_q, sx, sy], late2.at[whole_q, dx, dy], o)

    arrive("perm3z")
    perm_all[gy] = perm_col[...].reshape(16, 128)
    for i, o in enumerate(PLANE):
        send("perm3y", i, perm_all.at[gy], perm_all.at[gy], o)
    arrive("perm2")
    couplings(range(10), 2, 10, permit2.at[0], mask2, kx2, ky2, kz2, True)
    for i in reach(2, 10, 3):
        inverse2[i] = masked(permit2[1, i], i, 2, 10, mask2)[0]

    arrive("perm3y")

    def ahead(u):
        return jnp.concatenate([u[1:], u[:1]], axis=0)

    def behind(u):
        return jnp.concatenate([u[-1:], u[:-1]], axis=0)

    def steps_of(extent_y, extent_x, extent_z, shape):
        y, x, z = iota(shape, 0), iota(shape, 1), iota(shape, 2)
        return [
            (ahead, y < extent_y - 1), (behind, y > 0),
            (lambda u: roll(u, -1, 1), x < extent_x - 1), (lambda u: roll(u, 1, 1), x > 0),
            (lambda u: roll(u, -1, 2), z < extent_z - 1), (lambda u: roll(u, 1, 2), z > 0),
        ]

    shape3 = (16, 16, 128)
    pair3, x3, lane3 = iota(shape3, 0), iota(shape3, 1), iota(shape3, 2)
    upper3 = lane3 >= 64
    z3 = lane3 % 64

    def across(u):
        turned = roll(u, 64, 2)
        return jnp.where(upper3, ahead(turned), behind(turned))

    steps3 = [
        (lambda u: roll(u, 64, 2), None),
        (across, jnp.logical_or(jnp.logical_and(upper3, pair3 < 15), jnp.logical_and(lane3 < 64, pair3 > 0))),
        (lambda u: roll(u, -1, 1), x3 < 15), (lambda u: roll(u, 1, 1), x3 > 0),
        (lambda u: roll(u, -1, 2), z3 < 63), (lambda u: roll(u, 1, 2), z3 > 0),
    ]

    def prepare(e, steps, cells):
        couple, total = [], None
        for shift, there in steps:
            k = e + shift(e)
            term = k if there is None else jnp.where(there, k, e)
            couple.append(k if there is None else jnp.where(there, k, 0.0))
            total = term if total is None else total + term
        inverse = 1.0 / total if cells is None else jnp.where(cells, 1.0 / total, 0.0)
        return couple, inverse

    def sum_around(u, steps, couple):
        total = None
        for (shift, _), k in zip(steps, couple):
            total = k * shift(u) if total is None else total + k * shift(u)
        return total

    pack3 = jnp.where(z_out == (z_in % 64) // 2, 1.0, 0.0).astype(F32)
    pack4 = jnp.where(z_out == z_in // 2, 1.0, 0.0).astype(F32)
    spread4 = jnp.where(jnp.logical_and(z_in == (z_out % 64) // 2, z_in < 32), 1.0, 0.0).astype(F32)
    spread5 = jnp.where(jnp.logical_and(z_in == z_out // 2, z_in < 16), 1.0, 0.0).astype(F32)

    def coarsen3(u):
        stage3[...] = mix(u.reshape(256, 128), pack3).reshape(16, 16, 128)
        return stage3[:, pl.ds(0, 8, stride=2), :] + stage3[:, pl.ds(1, 8, stride=2), :]

    def coarsen4(u):
        pairs = jnp.concatenate([u[2 * i : 2 * i + 1] + u[2 * i + 1 : 2 * i + 2] for i in range(8)], axis=0)
        stage4[...] = mix(pairs.reshape(64, 128), pack4).reshape(8, 8, 128)
        stage5[...] = jnp.zeros_like(stage5)
        stage5[:, pl.ds(0, 4), :] = stage4[:, pl.ds(0, 4, stride=2), :] + stage4[:, pl.ds(1, 4, stride=2), :]
        return stage5[...]

    shape4, shape5 = (16, 8, 128), (8, 8, 128)
    steps4, steps5 = steps_of(16, 8, 32, shape4), steps_of(8, 4, 16, shape5)
    e3 = perm_all[...]
    k3, inverse3 = prepare(e3, steps3, None)
    for j in range(6):
        couple3[j] = k3[j]
    couple3[6] = inverse3
    e4 = 0.125 * coarsen3(e3)
    k4, inverse4 = prepare(e4, steps4, iota(shape4, 2) < 32)
    e5 = 0.125 * coarsen4(e4)
    k5, inverse5 = prepare(e5, steps5, jnp.logical_and(iota(shape5, 2) < 16, iota(shape5, 1) < 4))
    even3 = (x3 + z3 + lane3 // 64) % 2 == 0
    even4 = (iota(shape4, 0) + iota(shape4, 1) + iota(shape4, 2)) % 2 == 0
    even5 = (iota(shape5, 0) + iota(shape5, 1) + iota(shape5, 2)) % 2 == 0

    arrive("right3z")
    right_all[gy] = right_col[...].reshape(16, 128)
    for i, o in enumerate(PLANE):
        send("right3y", i, right_all.at[gy], right_all.at[gy], o)
    arrive("late2")
    arrive("right3y")

    g3 = right_all[...]
    first3 = g3 * inverse3
    dark3 = (g3 + sum_around(first3, steps3, k3)) * inverse3
    rest3 = sum_around(dark3, steps3, k3)
    g4 = 0.5 * coarsen3(jnp.where(even3, rest3, 0.0))
    first4 = g4 * inverse4
    dark4 = (g4 + sum_around(first4, steps4, k4)) * inverse4
    rest4 = sum_around(dark4, steps4, k4)
    g5 = 0.5 * coarsen4(jnp.where(even4, rest4, 0.0))
    light5 = g5 * inverse5
    dark5 = (g5 + sum_around(light5, steps5, k5)) * inverse5
    for _ in range(3):
        light5 = (g5 + sum_around(dark5, steps5, k5)) * inverse5
        dark5 = (g5 + sum_around(light5, steps5, k5)) * inverse5
    u5 = jnp.where(even5, light5, dark5)
    wide5 = mix(u5.reshape(64, 128), spread5).reshape(8, 8, 128)[:, :4]
    stage4[:, pl.ds(0, 4, stride=2), :] = wide5
    stage4[:, pl.ds(1, 4, stride=2), :] = wide5
    c4 = jnp.concatenate([stage4[i // 2 : i // 2 + 1] for i in range(16)], axis=0)
    light4 = (g4 + sum_around(dark4 + c4, steps4, k4)) * inverse4
    end4 = (g4 + sum_around(light4, steps4, k4)) * inverse4
    u4 = jnp.where(even4, light4, end4)
    up4[...] = u4

    def plane_of(step):
        return lax.rem(gy + (step + PEERS_Y), PEERS_Y)

    near4 = mix(jnp.concatenate([up4[plane_of(p)] for p in range(-3, 5)], axis=0), spread4).reshape(8, 8, 128)
    stage3[pl.ds(0, 8), pl.ds(0, 8, stride=2), :] = near4
    stage3[pl.ds(0, 8), pl.ds(1, 8, stride=2), :] = near4
    up3[...] = g3 + rest3
    upper_plane = iota((16, 128), 1) >= 64
    even_plane = (iota((16, 128), 0) + iota((16, 128), 1) + iota((16, 128), 1) // 64) % 2 == 0

    def around3(u, p):
        at = plane_of(p)
        here = u[p]
        beyond = jnp.where(upper_plane, roll(u[p + 1], 64, 1), roll(u[p - 1], 64, 1))
        total = couple3[0, at] * roll(here, 64, 1) + couple3[1, at] * beyond
        total = total + (couple3[2, at] * roll(here, -1, 0) + couple3[3, at] * roll(here, 1, 0))
        return total + (couple3[4, at] * roll(here, -1, 1) + couple3[5, at] * roll(here, 1, 1))

    corr3 = {p: stage3[p + 3] for p in range(-3, 4)}
    light3 = {p: (up3[plane_of(p)] + around3(corr3, p)) * couple3[6, plane_of(p)] for p in range(-2, 3)}
    end3 = {}
    for p in range(-1, 2):
        dark = (right_all[plane_of(p)] + around3(light3, p)) * couple3[6, plane_of(p)]
        end3[p] = jnp.where(even_plane, light3[p], dark)

    spread3 = jnp.concatenate(
        [
            jnp.where(z_in == z_out // 2, 1.0, 0.0).astype(F32),
            jnp.where(z_in == z_out // 2 + 64, 1.0, 0.0).astype(F32),
        ],
        axis=1,
    )
    for dy, base in ((0, 0), (1, 4), (-1, 12)):
        turned = pltpu.roll(end3[dy], lax.rem(PEERS_X - gx, PEERS_X), 0)
        wide = mix(turned, spread3)
        for cell, row in ((0, 0), (1, 2), (2, 4), (14, 6), (15, 8)):
            low = jnp.broadcast_to(wide[cell : cell + 1, :128], (2, 128))
            high = jnp.broadcast_to(wide[cell : cell + 1, 128:], (2, 128))
            for i in (row, row + 1):
                stage2[i, pl.ds(base, 2), :] = low
                stage2[i, pl.ds(base + 2, 2), :] = high
    for i in range(10):
        half2[i] = masked(late2[1, i] + stage2[i], i, 2, 10, mask2)[0]
    for i in reach(2, 10, 3):
        red2[i] = (late2[0, i] + around(half2, i, 10, kx2, ky2, kz2)) * inverse2[i]
    even2 = (iota((16, 128), 0) + iota((16, 128), 1)) % 2
    u2 = {}
    for i in reach(2, 10, 2):
        dark = (late2[0, i] + around(red2, i, 10, kx2, ky2, kz2)) * inverse2[i]
        u2[i] = jnp.where(even2 == i % 2, red2[i], dark)

    spread2 = jnp.where(iota((128, 256), 0) == iota((128, 256), 1) // 2, 1.0, 0.0).astype(F32)
    order2 = (0, 1, 2, 3, 8, 9)
    for j, cell in enumerate(order2):
        plane = u2[cell]
        stage1[j, pl.ds(0, 4, stride=2), :] = plane[:4]
        stage1[j, pl.ds(1, 4, stride=2), :] = plane[:4]
        for row, source in ((8, 4), (10, 5), (20, 14), (22, 15)):
            stage1[j, pl.ds(row, 2), :] = jnp.broadcast_to(plane[source : source + 1], (2, 128))
    wide2 = mix(stage1[pl.ds(0, 6)].reshape(144, 128), spread2)
    for j, cell in enumerate(order2):
        for i in {0: (0, 1), 1: (2, 3), 2: (4, 5), 3: (6,), 8: (15,), 9: (16, 17)}[cell]:
            part = black1[i] + wide2[24 * j : 24 * j + 24]
            half1[i] = masked(part, i, 4, 18, mask1)[0]
    for i in reach(4, 18, 2):
        red1[i] = (right1[i] + around(half1, i, 18, kx1, ky1, kz1)) * inv1[i]
    u1 = {}
    for i in reach(4, 18, 1):
        dark = (right1[i] + around(red1, i, 18, kx1, ky1, kz1)) * inv1[i]
        u1[i] = jnp.where(odd1 == i % 2, red1[i], dark)

    order1 = (0, 1, 2, 3, 4, 17)
    halo_lane = jnp.where(z_out < 64, z_out // 2, 64 + z_out // 2)
    spread_halo = jnp.where(z_in == halo_lane, 1.0, 0.0).astype(F32)
    for j, cell in enumerate(order1):
        low, high = u1[cell][:, :128], u1[cell][:, 128:]
        for part, plane in ((0, jnp.where(beside == 1, low, high)), (1, jnp.where(beside == 1, high, low))):
            stage6[part, j, pl.ds(0, 8, stride=2), :] = plane[:8]
            stage6[part, j, pl.ds(1, 8, stride=2), :] = plane[:8]
            stage6[part, j, pl.ds(16, 2), :] = jnp.broadcast_to(plane[8:9], (2, 128))
            stage6[part, j, pl.ds(22, 2), :] = jnp.broadcast_to(plane[23:24], (2, 128))
    wide1 = mix(stage6[0].reshape(144, 128), spread2)
    edge1 = mix(stage6[1].reshape(144, 128), spread_halo)
    for j, cell in enumerate(order1):
        for i in {0: (0, 1), 1: (2, 3), 2: (4, 5), 3: (6, 7), 4: (8, 9), 17: (14, 15)}[cell]:
            part = jnp.concatenate([wide1[24 * j : 24 * j + 24], edge1[24 * j : 24 * j + 24]], axis=1)
            half0[i] = masked(black0[i] + part, i, 8, 16, mask0)[0]
    for i in reach(8, 16, 1):
        red0[i] = (2.0 * charge0[i] + around(half0, i, 16, kx0, ky0, kz0)) * inv0[i]
    for i in range(8):
        dark = (2.0 * charge0[i] + around(red0, i, 16, kx0, ky0, kz0)) * inv0[i]
        out_ref[i] = jnp.where(odd0 == i % 2, red0[i, :16, :256], dark[:16, :256])

    for group in copies.values():
        for copy in group:
            copy.wait_send()


def per_device(charge, permittivity):
    def vmem(*shape):
        return pltpu.VMEM(shape, F32)

    fine, middle, coarse = (16, 24, 384), (18, 24, 256), (10, 16, 128)
    scratch = [vmem(*fine) for _ in range(9)] + [vmem(4, 16, 128), vmem(2, 24, 384), vmem(2, 24, 384)]
    scratch += [vmem(*middle) for _ in range(9)] + [vmem(8, 24, 128)]
    scratch += [vmem(2, *coarse)] + [vmem(*coarse) for _ in range(7)] + [vmem(2, *coarse), vmem(*coarse)]
    scratch += [vmem(16, 1, 128), vmem(16, 16, 128), vmem(16, 1, 128), vmem(16, 16, 128)]
    scratch += [vmem(16, 16, 128), vmem(8, 8, 128), vmem(8, 8, 128), vmem(2, 6, 24, 128)]
    scratch += [vmem(7, 16, 16, 128), vmem(16, 16, 128), vmem(16, 8, 128)]
    scratch += [pltpu.SemaphoreType.DMA((2,)), pltpu.SemaphoreType.DMA((TOTAL,)), pltpu.SemaphoreType.DMA((TOTAL,))]
    scratch += [pltpu.SemaphoreType.REGULAR((3,))]
    return pl.pallas_call(
        kernel,
        out_shape=jax.ShapeDtypeStruct(charge.shape, F32),
        in_specs=[pl.BlockSpec(memory_space=pl.ANY)] * 2,
        out_specs=pl.BlockSpec(memory_space=pltpu.VMEM),
        scratch_shapes=scratch,
        compiler_params=pltpu.CompilerParams(
            collective_id=0, has_side_effects=True, vmem_limit_bytes=55040 * 1024
        ),
        name="vcycle",
    )(charge, permittivity)


def solution(mesh):
    return jax.shard_map(
        per_device,
        mesh=mesh,
        in_specs=(P("gx", "gy", "gz"), P("gx", "gy", "gz")),
        out_specs=P("gx", "gy", "gz"),
        check_vma=False,
    )
```

```python
import jax
import jax.numpy as jnp
from jax import lax
from jax.experimental import pallas as pl
from jax.experimental.pallas import tpu as pltpu
from jax.sharding import PartitionSpec as P

MESH = pl.DeviceIdType.MESH
F32 = jnp.float32
PEERS_X = 16
PEERS_Y = 16

NEAR = [(a, b, c) for c in (0, 1) for a in (-1, 0, 1) for b in (-1, 0, 1) if (a, b, c) != (0, 0, 0)]
NEAR.sort(key=lambda o: (-abs(o[0]), -sum(abs(step) for step in o)))
SAME = [o for o in NEAR if o[2] == 0]
FAR = SAME + [(a, b, 0) for a in (-2, 2) for b in (-1, 0, 1)]
WIDE = NEAR + [(a, b, c) for c in (0, 1) for a in (-2, 2) for b in (-1, 0, 1)]
SIDE = [o for o in NEAR if o[0]]
RING = [(i, 0, 0) for i in sorted(range(-7, 9), key=lambda i: -abs(i)) if i]
PLANE = [(0, i, 0) for i in (6, -6, 2, -2, 5, 7, -5, -7, 8, 3, -3, 4, -4, 1, -1)]

COUNTS = {
    "charge0": len(NEAR), "perm0": len(NEAR), "charge0far": len(SIDE), "perm0far": len(SIDE), "perm1": len(WIDE),
    "right1": len(WIDE), "perm2": len(FAR), "perm3z": len(RING), "perm3y": len(PLANE), "right3z": len(RING),
    "right3y": len(PLANE), "late2": len(FAR),
}
BASE = {}
TOTAL = 0
for _key, _count in COUNTS.items():
    BASE[_key] = TOTAL
    TOTAL += _count


def iota(shape, dim):
    return lax.broadcasted_iota(jnp.int32, shape, dim)


def roll(value, shift, axis):
    return pltpu.roll(value, shift % value.shape[axis], axis)


def mix(left, right):
    if left.shape[0] % 16:
        return jnp.dot(left, right, precision=lax.Precision.HIGHEST, preferred_element_type=F32)
    ones, total = right.astype(jnp.bfloat16), None
    for _ in range(3):
        part = left.astype(jnp.bfloat16)
        left = left - part.astype(F32)
        term = jnp.dot(part, ones, preferred_element_type=F32)
        total = term if total is None else total + term
    return total


def halver(size, out):
    return jnp.where(iota((size, out), 0) // 2 == iota((size, out), 1), 1.0, 0.0).astype(F32)


def span(step, size, count, width):
    if step == 0:
        return pl.ds(0, size), pl.ds(0, size)
    if step > 0:
        return pl.ds(size - width, width), pl.ds(count - width, width)
    return pl.ds(0, width), pl.ds(size, width)


def kernel(
    charge_hbm, permit_hbm, out_ref,
    charge0, permit0, kx0, ky0, kz0, inv0, half0, black0, red0, stage0, edge_permit, edge_charge,
    permit1, kx1, ky1, kz1, inv1, right1, half1, black1, red1, stage1,
    permit2, kx2, ky2, kz2, right2, half2, black2, red2, late2, stage2,
    perm_col, perm_all, right_col, right_all, stage3, stage4, stage5, stage6, couple3, up3, up4,
    local_sem, send_sem, recv_sem, token_sem,
):
    gx, gy, gz = lax.axis_index("gx"), lax.axis_index("gy"), lax.axis_index("gz")

    def peer(o):
        return (
            lax.rem(gx + (o[0] + PEERS_X), PEERS_X),
            lax.rem(gy + (o[1] + PEERS_Y), PEERS_Y),
            (1 - gz) if o[2] else gz,
        )

    copies = {}

    def send(name, index, src, dst, o):
        slot = BASE[name] + index
        copy = pltpu.make_async_remote_copy(
            src_ref=src, dst_ref=dst, send_sem=send_sem.at[slot], recv_sem=recv_sem.at[slot],
            device_id=peer(o), device_id_type=MESH,
        )
        copy.start()
        copies.setdefault(name, []).append(copy)

    def arrive(name, skip=None):
        for index, copy in enumerate(copies[name]):
            if index != skip:
                copy.wait_recv()

    barrier = pltpu.get_barrier_semaphore()
    for o in NEAR:
        pl.semaphore_signal(barrier, inc=1, device_id=peer(o), device_id_type=MESH)
    own0 = (pl.ds(0, 8), pl.ds(0, 16), pl.ds(0, 256))
    fetch_permit = pltpu.make_async_copy(permit_hbm, permit0.at[own0], local_sem.at[0])
    fetch_charge = pltpu.make_async_copy(charge_hbm, charge0.at[own0], local_sem.at[1])
    fetch_permit.start()
    fetch_charge.start()
    half_256 = halver(256, 128)
    lane_half = pl.ds(pl.multiple_of(gz * 128, 128), 128)

    def coarsen0(rows):
        pairs = [rows[2 * i] + rows[2 * i + 1] for i in range(4)]
        stage0[...] = mix(jnp.concatenate(pairs, axis=0), half_256).reshape(4, 16, 128)
        return stage0[:, pl.ds(0, 8, stride=2), :] + stage0[:, pl.ds(1, 8, stride=2), :]

    def tell(turn):
        step = 2**turn
        for o in ((step, 0, 0), (-step, 0, 0), (0, step, 0), (0, -step, 0)):
            pl.semaphore_signal(token_sem.at[turn], inc=1, device_id=peer(o), device_id_type=MESH)

    def hear(turn):
        pl.semaphore_wait(token_sem.at[turn], 4)

    def send0(name, source, ref, reach, far):
        for i, o in enumerate(SIDE if far else NEAR):
            away = sum(abs(step) for step in o)
            width = reach + 1 - away
            sx, dx, target = pl.ds(0, 8), pl.ds(0, 8), ref
            if far and away == 3:
                continue
            if o[0]:
                last = 1 if away < 3 else 0
                rows = 1 if far else width - last
                start = (width - 1 if far else 0) if o[0] < 0 else 8 - (width if far else width - last)
                sx, dx = pl.ds(start, rows), pl.ds(start + 8, rows)
                if far and away == 2:
                    target, dx = (edge_permit if reach == 4 else edge_charge), pl.ds(0 if o[0] < 0 else 1, 1)
            sy, dy = span(o[1], 16, 24, width)
            if o[2]:
                sz, dz = pl.ds(pl.multiple_of((1 - gz) * 128, 128), 128), pl.ds(256, 128)
            else:
                sz, dz = pl.ds(0, 256), pl.ds(0, 256)
            send(name, i, source.at[sx, sy, sz], target.at[dx, dy, dz], o)

    pl.semaphore_wait(barrier, len(NEAR))
    tell(0)
    send0("perm0", permit_hbm, permit0, 4, False)
    send0("charge0", charge_hbm, charge0, 3, False)

    fetch_permit.wait()
    permit1[pl.ds(0, 4), pl.ds(0, 8), lane_half] = 0.125 * coarsen0([permit0[i, :16, :256] for i in range(8)])
    fetch_charge.wait()

    def send1(name, ref, reach, peers):
        for i, o in sorted(enumerate(WIDE), key=lambda pair: -abs(pair[1][0])):
            if o not in peers:
                continue
            away = abs(o[0])
            along = {0: 4, 1: 4, 2: reach - 4 - abs(o[1])}[away]
            across = {0: reach, 1: reach - 1, 2: reach - 5}[away]
            if away < 2:
                sx, dx = span(o[0], 4, 18, along)
            else:
                sx = pl.ds(4 - along, along) if o[0] > 0 else pl.ds(0, along)
                dx = pl.ds(14 - along, along) if o[0] > 0 else pl.ds(8, along)
            sy, dy = span(o[1], 8, 24, across)
            send(name, i, ref.at[sx, sy, lane_half], ref.at[dx, dy, lane_half], o)

    send1("perm1", permit1, 7, NEAR)
    hear(0)
    tell(1)
    send1("perm1", permit1, 7, WIDE[len(NEAR):])
    send0("perm0far", permit_hbm, permit0, 4, True)
    send0("charge0far", charge_hbm, charge0, 3, True)

    def inside_x(i, size, count):
        if i < size:
            return None
        ahead = i < (size + count) // 2
        blocks = (i - size) // size + 1 if ahead else (count - 1 - i) // size + 1
        return gx < PEERS_X - blocks if ahead else gx >= blocks

    def masked(value, i, size, count, mask):
        row_in = inside_x(i, size, count)
        keep = mask if row_in is None else jnp.logical_and(mask, row_in)
        return jnp.where(keep, value, 0.0), keep

    def inside_y(shape, own, ahead):
        row = iota(shape, 0)
        after = jnp.logical_and(jnp.logical_and(row >= own, row < ahead), gy < PEERS_Y - 1)
        return jnp.logical_or(row < own, jnp.logical_or(after, jnp.logical_and(row >= ahead, gy > 0)))

    def couplings(rows, size, count, permit, mask, kx, ky, kz, wrap):
        values = {}
        for i in rows:
            values[i] = masked(permit[i], i, size, count, mask)[0]
        shape = values[rows[0]].shape
        top = iota(shape, 1) == shape[1] - 1
        for i in rows:
            e = values[i]
            ky[i] = e + roll(e, -1, 0)
            along = e + roll(e, -1, 1)
            kz[i] = jnp.where(top, 0.0, along) if wrap else along
            after = (i + 1) % count
            if after in values:
                kx[i] = e + values[after]
        return values

    def diagonal(i, count, e, kx, ky, kz, wrap):
        y, z = ky[i], kz[i]
        total = kx[i] + kx[(i - 1) % count] + (y + roll(y, 1, 0)) + (z + roll(z, 1, 1))
        if wrap:
            lane = iota(e.shape, 1)
            ends = jnp.logical_or(lane == 0, lane == e.shape[1] - 1)
            total = total + jnp.where(ends, e, 0.0)
        return total

    def around(u, i, count, kx, ky, kz):
        here, y, z = u[i], ky[i], kz[i]
        before = (i - 1) % count
        total = kx[i] * u[(i + 1) % count] + kx[before] * u[before]
        total = total + (y * roll(here, -1, 0) + roll(y * here, 1, 0))
        return total + (z * roll(here, -1, 1) + roll(z * here, 1, 1))

    def reach(size, count, width):
        return list(range(size + width)) + list(range(count - width, count))

    hear(1)
    tell(2)

    z_in, z_out = iota((128, 128), 0), iota((128, 128), 1)
    pack_low = jnp.where(z_out == z_in // 2, 1.0, 0.0).astype(F32)
    pack_high = jnp.where(z_out == z_in // 2 + 64, 1.0, 0.0).astype(F32)

    def coarsen2(first, second):
        both = first + second
        low, high = both[0:1] + both[1:2], both[2:3] + both[3:4]
        return mix(low, pack_low) + mix(high, pack_high)

    copies["perm1"][NEAR.index((0, 0, 1))].wait_recv()
    near1 = [permit1[i, pl.ds(0, 8), :] for i in range(4)]
    stage3[0] = mix(jnp.concatenate([near1[0] + near1[1], near1[2] + near1[3]], axis=0), half_256)
    own2 = [stage3[0, pl.ds(8 * i, 4, stride=2), :] + stage3[0, pl.ds(8 * i + 1, 4, stride=2), :] for i in range(2)]
    perm_col[gx] = 0.015625 * coarsen2(own2[0], own2[1])

    arrive("perm0")
    lane0 = iota((24, 384), 1)
    beside = jnp.where(gz == 0, 1, 0)
    mask_z = jnp.logical_or(
        lane0 < 256,
        jnp.logical_or(jnp.logical_and(lane0 < 320, beside == 1), jnp.logical_and(lane0 >= 320, beside == 0)),
    )
    mask0 = jnp.logical_and(inside_y((24, 384), 16, 20), mask_z)
    e0 = couplings(reach(8, 16, 3), 8, 16, permit0, mask0, kx0, ky0, kz0, False)

    def diagonal0(i, e):
        keep = masked(e, i, 8, 16, mask0)[1]
        inv0[i] = jnp.where(keep, 1.0 / diagonal(i, 16, e, kx0, ky0, kz0, False), 0.0)

    def first0(i, charge):
        half0[i] = (2.0 * charge) * inv0[i]

    def second0(i):
        black0[i] = half0[i] + around(half0, i, 16, kx0, ky0, kz0) * inv0[i]

    for i in reach(8, 16, 2):
        diagonal0(i, e0[i])
    arrive("charge0")
    for i in reach(8, 16, 2):
        first0(i, charge0[i])
    for i in reach(8, 16, 1):
        second0(i)
    odd0 = (iota((16, 256), 0) + iota((16, 256), 1)) % 2
    left0 = []
    for i in range(8):
        rest = around(black0, i, 16, kx0, ky0, kz0)[:16, :256]
        left0.append(jnp.where(odd0 == i % 2, rest, 0.0))
    right1[pl.ds(0, 4), pl.ds(0, 8), lane_half] = 0.5 * coarsen0(left0)
    send1("right1", right1, 6, WIDE)
    hear(2)
    for i, o in enumerate(RING):
        send("perm3z", i, perm_col.at[gx], perm_col.at[gx], o)

    arrive("perm1", NEAR.index((0, 0, 1)))
    mask1 = inside_y((24, 256), 8, 16)
    e1 = couplings(range(18), 4, 18, permit1, mask1, kx1, ky1, kz1, True)

    def coarsen1(rows, ref, cells):
        half = len(rows) // 2
        pairs = [rows[2 * i] + rows[2 * i + 1] for i in range(half)]
        stage1[pl.ds(0, half)] = mix(jnp.concatenate(pairs, axis=0), half_256).reshape(half, 24, 128)
        for j, cell in enumerate(cells):
            ref[cell, pl.ds(0, 8), :] = stage1[j, pl.ds(0, 8, stride=2), :] + stage1[j, pl.ds(1, 8, stride=2), :]
            ref[cell, pl.ds(12, 4), :] = stage1[j, pl.ds(16, 4, stride=2), :] + stage1[j, pl.ds(17, 4, stride=2), :]

    cells2 = (0, 1, 2, 3, 4, 7, 8, 9)
    coarsen1([0.125 * e1[i] for i in (0, 1, 2, 3, 4, 5, 6, 7, 8, 9, 12, 13, 14, 15, 16, 17)], stage2, cells2)
    mask2 = inside_y((16, 128), 4, 8)
    e2 = couplings(cells2, 2, 10, stage2, mask2, kx2, ky2, kz2, True)
    inverse2 = {}
    for i in reach(2, 10, 2):
        keep = masked(e2[i], i, 2, 10, mask2)[1]
        inverse2[i] = jnp.where(keep, 1.0 / diagonal(i, 10, e2[i], kx2, ky2, kz2, True), 0.0)
    for i in range(2):
        permit2[0, i, pl.ds(0, 4), :] = e2[i][:4]
        permit2[1, i, pl.ds(0, 4), :] = inverse2[i][:4]

    def span_far(step):
        if step == 0:
            return pl.ds(0, 2), pl.ds(0, 2)
        start = {1: 8, 2: 6, -1: 2, -2: 4}[step]
        return pl.ds(0, 2), pl.ds(start, 2)

    whole_q = pl.ds(0, 2)
    for i, o in enumerate(FAR):
        (sx, dx), (sy, dy) = span_far(o[0]), span(o[1], 4, 16, 4)
        send("perm2", i, permit2.at[whole_q, sx, sy], permit2.at[whole_q, dx, dy], o)
    for i in reach(4, 18, 6):
        keep = masked(e1[i], i, 4, 18, mask1)[1]
        inv1[i] = jnp.where(keep, 1.0 / diagonal(i, 18, e1[i], kx1, ky1, kz1, True), 0.0)

    arrive("perm0far")
    arrive("charge0far")
    edge = jnp.logical_or(iota((24, 384), 0) >= 16, lane0 >= 256)
    far_permit = {i: permit0[i] for i in range(8, 16)}
    far_permit[10] = jnp.where(edge, edge_permit[0], far_permit[10])
    far_permit[13] = jnp.where(edge, edge_permit[1], far_permit[13])
    far_charge = {i: charge0[i] for i in (8, 9, 10, 13, 14, 15)}
    far_charge[9] = jnp.where(edge, edge_charge[0], far_charge[9])
    far_charge[14] = jnp.where(edge, edge_charge[1], far_charge[14])
    e0 = couplings(range(8, 16), 8, 16, far_permit, mask0, kx0, ky0, kz0, False)
    for i in (8, 9, 10, 13, 14, 15):
        diagonal0(i, e0[i])
    for i in (8, 9, 10, 13, 14, 15):
        first0(i, far_charge[i])
    for i in (8, 9, 14, 15):
        second0(i)

    arrive("right1")
    for i in reach(4, 18, 6):
        half1[i] = right1[i] * inv1[i]
    for i in reach(4, 18, 5):
        black1[i] = half1[i] + around(half1, i, 18, kx1, ky1, kz1) * inv1[i]
    odd1 = (iota((24, 256), 0) + iota((24, 256), 1)) % 2
    left1 = []
    for i in reach(4, 18, 4):
        left1.append(jnp.where(odd1 == i % 2, 0.5 * around(black1, i, 18, kx1, ky1, kz1), 0.0))
    coarsen1(left1, right2, (0, 1, 2, 3, 8, 9))

    for i in reach(2, 10, 2):
        half2[i] = right2[i] * inverse2[i]
    for i in reach(2, 10, 1):
        black2[i] = half2[i] + around(half2, i, 10, kx2, ky2, kz2) * inverse2[i]
    odd2 = (iota((4, 128), 0) + iota((4, 128), 1)) % 2
    left2 = []
    for i in range(2):
        rest = around(black2, i, 10, kx2, ky2, kz2)[:4]
        left2.append(jnp.where(odd2 == i % 2, rest, 0.0))
    right_col[gx] = 0.5 * coarsen2(left2[0], left2[1])
    for i, o in enumerate(RING):
        send("right3z", i, right_col.at[gx], right_col.at[gx], o)
    for i in range(2):
        late2[0, i, pl.ds(0, 4), :] = right2[i, :4]
        late2[1, i, pl.ds(0, 4), :] = black2[i, :4]
    for i, o in enumerate(FAR):
        (sx, dx), (sy, dy) = span_far(o[0]), span(o[1], 4, 16, 4)
        send("late2", i, late2.at[whole_q, sx, sy], late2.at[whole_q, dx, dy], o)

    arrive("perm3z")
    perm_all[gy] = perm_col[...].reshape(16, 128)
    for i, o in enumerate(PLANE):
        send("perm3y", i, perm_all.at[gy], perm_all.at[gy], o)
    arrive("perm2")
    couplings(range(10), 2, 10, permit2.at[0], mask2, kx2, ky2, kz2, True)
    for i in reach(2, 10, 3):
        inverse2[i] = masked(permit2[1, i], i, 2, 10, mask2)[0]

    arrive("perm3y")

    def ahead(u):
        return jnp.concatenate([u[1:], u[:1]], axis=0)

    def behind(u):
        return jnp.concatenate([u[-1:], u[:-1]], axis=0)

    def steps_of(extent_y, extent_x, extent_z, shape):
        y, x, z = iota(shape, 0), iota(shape, 1), iota(shape, 2)
        return [
            (ahead, y < extent_y - 1), (behind, y > 0),
            (lambda u: roll(u, -1, 1), x < extent_x - 1), (lambda u: roll(u, 1, 1), x > 0),
            (lambda u: roll(u, -1, 2), z < extent_z - 1), (lambda u: roll(u, 1, 2), z > 0),
        ]

    shape3 = (16, 16, 128)
    pair3, x3, lane3 = iota(shape3, 0), iota(shape3, 1), iota(shape3, 2)
    upper3 = lane3 >= 64
    z3 = lane3 % 64

    def across(u):
        turned = roll(u, 64, 2)
        return jnp.where(upper3, ahead(turned), behind(turned))

    steps3 = [
        (lambda u: roll(u, 64, 2), None),
        (across, jnp.logical_or(jnp.logical_and(upper3, pair3 < 15), jnp.logical_and(lane3 < 64, pair3 > 0))),
        (lambda u: roll(u, -1, 1), x3 < 15), (lambda u: roll(u, 1, 1), x3 > 0),
        (lambda u: roll(u, -1, 2), z3 < 63), (lambda u: roll(u, 1, 2), z3 > 0),
    ]

    def prepare(e, steps, cells):
        couple, total = [], None
        for shift, there in steps:
            k = e + shift(e)
            term = k if there is None else jnp.where(there, k, e)
            couple.append(k if there is None else jnp.where(there, k, 0.0))
            total = term if total is None else total + term
        inverse = 1.0 / total if cells is None else jnp.where(cells, 1.0 / total, 0.0)
        return couple, inverse

    def sum_around(u, steps, couple):
        total = None
        for (shift, _), k in zip(steps, couple):
            total = k * shift(u) if total is None else total + k * shift(u)
        return total

    pack3 = jnp.where(z_out == (z_in % 64) // 2, 1.0, 0.0).astype(F32)
    pack4 = jnp.where(z_out == z_in // 2, 1.0, 0.0).astype(F32)
    spread4 = jnp.where(jnp.logical_and(z_in == (z_out % 64) // 2, z_in < 32), 1.0, 0.0).astype(F32)
    spread5 = jnp.where(jnp.logical_and(z_in == z_out // 2, z_in < 16), 1.0, 0.0).astype(F32)

    def coarsen3(u):
        stage3[...] = mix(u.reshape(256, 128), pack3).reshape(16, 16, 128)
        return stage3[:, pl.ds(0, 8, stride=2), :] + stage3[:, pl.ds(1, 8, stride=2), :]

    def coarsen4(u):
        pairs = jnp.concatenate([u[2 * i : 2 * i + 1] + u[2 * i + 1 : 2 * i + 2] for i in range(8)], axis=0)
        stage4[...] = mix(pairs.reshape(64, 128), pack4).reshape(8, 8, 128)
        stage5[...] = jnp.zeros_like(stage5)
        stage5[:, pl.ds(0, 4), :] = stage4[:, pl.ds(0, 4, stride=2), :] + stage4[:, pl.ds(1, 4, stride=2), :]
        return stage5[...]

    shape4, shape5 = (16, 8, 128), (8, 8, 128)
    steps4, steps5 = steps_of(16, 8, 32, shape4), steps_of(8, 4, 16, shape5)
    e3 = perm_all[...]
    k3, inverse3 = prepare(e3, steps3, None)
    for j in range(6):
        couple3[j] = k3[j]
    couple3[6] = inverse3
    e4 = 0.125 * coarsen3(e3)
    k4, inverse4 = prepare(e4, steps4, iota(shape4, 2) < 32)
    e5 = 0.125 * coarsen4(e4)
    k5, inverse5 = prepare(e5, steps5, jnp.logical_and(iota(shape5, 2) < 16, iota(shape5, 1) < 4))
    even3 = (x3 + z3 + lane3 // 64) % 2 == 0
    even4 = (iota(shape4, 0) + iota(shape4, 1) + iota(shape4, 2)) % 2 == 0
    even5 = (iota(shape5, 0) + iota(shape5, 1) + iota(shape5, 2)) % 2 == 0

    left_over = ("right3z", "late2", "perm3y", "right3y")
    for name, group in copies.items():
        if name not in left_over:
            for copy in group:
                copy.wait_send()
    arrive("right3z")
    right_all[gy] = right_col[...].reshape(16, 128)
    for i, o in enumerate(PLANE):
        send("right3y", i, right_all.at[gy], right_all.at[gy], o)
    arrive("late2")
    for name in left_over:
        for copy in copies[name]:
            copy.wait_send()
    arrive("right3y")

    g3 = right_all[...]
    first3 = g3 * inverse3
    dark3 = (g3 + sum_around(first3, steps3, k3)) * inverse3
    rest3 = sum_around(dark3, steps3, k3)
    g4 = 0.5 * coarsen3(jnp.where(even3, rest3, 0.0))
    first4 = g4 * inverse4
    dark4 = (g4 + sum_around(first4, steps4, k4)) * inverse4
    rest4 = sum_around(dark4, steps4, k4)
    g5 = 0.5 * coarsen4(jnp.where(even4, rest4, 0.0))
    light5 = g5 * inverse5
    dark5 = (g5 + sum_around(light5, steps5, k5)) * inverse5
    for _ in range(3):
        light5 = (g5 + sum_around(dark5, steps5, k5)) * inverse5
        dark5 = (g5 + sum_around(light5, steps5, k5)) * inverse5
    u5 = jnp.where(even5, light5, dark5)
    wide5 = mix(u5.reshape(64, 128), spread5).reshape(8, 8, 128)[:, :4]
    stage4[:, pl.ds(0, 4, stride=2), :] = wide5
    stage4[:, pl.ds(1, 4, stride=2), :] = wide5
    c4 = jnp.concatenate([stage4[i // 2 : i // 2 + 1] for i in range(16)], axis=0)
    light4 = (g4 + sum_around(dark4 + c4, steps4, k4)) * inverse4
    end4 = (g4 + sum_around(light4, steps4, k4)) * inverse4
    u4 = jnp.where(even4, light4, end4)
    up4[...] = u4

    def plane_of(step):
        return lax.rem(gy + (step + PEERS_Y), PEERS_Y)

    near4 = mix(jnp.concatenate([up4[plane_of(p)] for p in range(-3, 5)], axis=0), spread4).reshape(8, 8, 128)
    stage3[pl.ds(0, 8), pl.ds(0, 8, stride=2), :] = near4
    stage3[pl.ds(0, 8), pl.ds(1, 8, stride=2), :] = near4
    up3[...] = g3 + rest3
    upper_plane = iota((16, 128), 1) >= 64
    even_plane = (iota((16, 128), 0) + iota((16, 128), 1) + iota((16, 128), 1) // 64) % 2 == 0

    def around3(u, p):
        at = plane_of(p)
        here = u[p]
        beyond = jnp.where(upper_plane, roll(u[p + 1], 64, 1), roll(u[p - 1], 64, 1))
        total = couple3[0, at] * roll(here, 64, 1) + couple3[1, at] * beyond
        total = total + (couple3[2, at] * roll(here, -1, 0) + couple3[3, at] * roll(here, 1, 0))
        return total + (couple3[4, at] * roll(here, -1, 1) + couple3[5, at] * roll(here, 1, 1))

    corr3 = {p: stage3[p + 3] for p in range(-3, 4)}
    light3 = {p: (up3[plane_of(p)] + around3(corr3, p)) * couple3[6, plane_of(p)] for p in range(-2, 3)}
    end3 = {}
    for p in range(-1, 2):
        dark = (right_all[plane_of(p)] + around3(light3, p)) * couple3[6, plane_of(p)]
        end3[p] = jnp.where(even_plane, light3[p], dark)

    spread3 = jnp.concatenate(
        [
            jnp.where(z_in == z_out // 2, 1.0, 0.0).astype(F32),
            jnp.where(z_in == z_out // 2 + 64, 1.0, 0.0).astype(F32),
        ],
        axis=1,
    )
    for dy, base in ((0, 0), (1, 4), (-1, 12)):
        turned = pltpu.roll(end3[dy], lax.rem(PEERS_X - gx, PEERS_X), 0)
        wide = mix(turned, spread3)
        for cell, row in ((0, 0), (1, 2), (2, 4), (14, 6), (15, 8)):
            low = jnp.broadcast_to(wide[cell : cell + 1, :128], (2, 128))
            high = jnp.broadcast_to(wide[cell : cell + 1, 128:], (2, 128))
            for i in (row, row + 1):
                stage2[i, pl.ds(base, 2), :] = low
                stage2[i, pl.ds(base + 2, 2), :] = high
    for i in range(10):
        half2[i] = masked(late2[1, i] + stage2[i], i, 2, 10, mask2)[0]
    for i in reach(2, 10, 3):
        red2[i] = (late2[0, i] + around(half2, i, 10, kx2, ky2, kz2)) * inverse2[i]
    even2 = (iota((16, 128), 0) + iota((16, 128), 1)) % 2
    u2 = {}
    for i in reach(2, 10, 2):
        dark = (late2[0, i] + around(red2, i, 10, kx2, ky2, kz2)) * inverse2[i]
        u2[i] = jnp.where(even2 == i % 2, red2[i], dark)

    spread2 = jnp.where(iota((128, 256), 0) == iota((128, 256), 1) // 2, 1.0, 0.0).astype(F32)
    order2 = (0, 1, 2, 3, 8, 9)
    for j, cell in enumerate(order2):
        plane = u2[cell]
        stage1[j, pl.ds(0, 4, stride=2), :] = plane[:4]
        stage1[j, pl.ds(1, 4, stride=2), :] = plane[:4]
        for row, source in ((8, 4), (10, 5), (20, 14), (22, 15)):
            stage1[j, pl.ds(row, 2), :] = jnp.broadcast_to(plane[source : source + 1], (2, 128))
    wide2 = mix(stage1[pl.ds(0, 6)].reshape(144, 128), spread2)
    for j, cell in enumerate(order2):
        for i in {0: (0, 1), 1: (2, 3), 2: (4, 5), 3: (6,), 8: (15,), 9: (16, 17)}[cell]:
            part = black1[i] + wide2[24 * j : 24 * j + 24]
            half1[i] = masked(part, i, 4, 18, mask1)[0]
    for i in reach(4, 18, 2):
        red1[i] = (right1[i] + around(half1, i, 18, kx1, ky1, kz1)) * inv1[i]
    u1 = {}
    for i in reach(4, 18, 1):
        dark = (right1[i] + around(red1, i, 18, kx1, ky1, kz1)) * inv1[i]
        u1[i] = jnp.where(odd1 == i % 2, red1[i], dark)

    order1 = (0, 1, 2, 3, 4, 17)
    halo_lane = jnp.where(z_out < 64, z_out // 2, 64 + z_out // 2)
    spread_halo = jnp.where(z_in == halo_lane, 1.0, 0.0).astype(F32)
    for j, cell in enumerate(order1):
        low, high = u1[cell][:, :128], u1[cell][:, 128:]
        for part, plane in ((0, jnp.where(beside == 1, low, high)), (1, jnp.where(beside == 1, high, low))):
            stage6[part, j, pl.ds(0, 8, stride=2), :] = plane[:8]
            stage6[part, j, pl.ds(1, 8, stride=2), :] = plane[:8]
            stage6[part, j, pl.ds(16, 2), :] = jnp.broadcast_to(plane[8:9], (2, 128))
            stage6[part, j, pl.ds(22, 2), :] = jnp.broadcast_to(plane[23:24], (2, 128))
    wide1 = mix(stage6[0].reshape(144, 128), spread2)
    edge1 = mix(stage6[1].reshape(144, 128), spread_halo)
    for j, cell in enumerate(order1):
        for i in {0: (0, 1), 1: (2, 3), 2: (4, 5), 3: (6, 7), 4: (8, 9), 17: (14, 15)}[cell]:
            part = jnp.concatenate([wide1[24 * j : 24 * j + 24], edge1[24 * j : 24 * j + 24]], axis=1)
            half0[i] = masked(black0[i] + part, i, 8, 16, mask0)[0]
    for i in reach(8, 16, 1):
        red0[i] = (2.0 * charge0[i] + around(half0, i, 16, kx0, ky0, kz0)) * inv0[i]
    for i in range(8):
        dark = (2.0 * charge0[i] + around(red0, i, 16, kx0, ky0, kz0)) * inv0[i]
        out_ref[i] = jnp.where(odd0 == i % 2, red0[i, :16, :256], dark[:16, :256])


def per_device(charge, permittivity):
    def vmem(*shape):
        return pltpu.VMEM(shape, F32)

    fine, middle, coarse = (16, 24, 384), (18, 24, 256), (10, 16, 128)
    scratch = [vmem(*fine) for _ in range(9)] + [vmem(4, 16, 128), vmem(2, 24, 384), vmem(2, 24, 384)]
    scratch += [vmem(*middle) for _ in range(9)] + [vmem(8, 24, 128)]
    scratch += [vmem(2, *coarse)] + [vmem(*coarse) for _ in range(7)] + [vmem(2, *coarse), vmem(*coarse)]
    scratch += [vmem(16, 1, 128), vmem(16, 16, 128), vmem(16, 1, 128), vmem(16, 16, 128)]
    scratch += [vmem(16, 16, 128), vmem(8, 8, 128), vmem(8, 8, 128), vmem(2, 6, 24, 128)]
    scratch += [vmem(7, 16, 16, 128), vmem(16, 16, 128), vmem(16, 8, 128)]
    scratch += [pltpu.SemaphoreType.DMA((2,)), pltpu.SemaphoreType.DMA((TOTAL,)), pltpu.SemaphoreType.DMA((TOTAL,))]
    scratch += [pltpu.SemaphoreType.REGULAR((3,))]
    return pl.pallas_call(
        kernel,
        out_shape=jax.ShapeDtypeStruct(charge.shape, F32),
        in_specs=[pl.BlockSpec(memory_space=pl.ANY)] * 2,
        out_specs=pl.BlockSpec(memory_space=pltpu.VMEM),
        scratch_shapes=scratch,
        compiler_params=pltpu.CompilerParams(
            collective_id=0, has_side_effects=True, vmem_limit_bytes=55040 * 1024
        ),
        name="vcycle",
    )(charge, permittivity)


def solution(mesh):
    return jax.shard_map(
        per_device,
        mesh=mesh,
        in_specs=(P("gx", "gy", "gz"), P("gx", "gy", "gz")),
        out_specs=P("gx", "gy", "gz"),
        check_vma=False,
    )
```
